32 devices in a mesh: row: 2 (over y), col: 16 (over z, x, core).
Axes of the slice: x: 2, y: 2, z: 4, core: 2. Of those that a mesh axis runs over, the one named last changes fastest.
Arguments:
- first_factor_strip: bfloat16 [1024, 2048], P('row', 'col'), may hold values from -16 to 16
- second_factor_strip: bfloat16 [2048, 6144], P('row', 'col'), may hold values from -0.125 to 0.125
- first_factor_support: int32 [8, 16], P('row', 'col'), may hold values 0 or 1
- second_factor_support: int32 [16, 48], P('row', 'col'), may hold values 0 or 1
- retained_blocks: int32 [8, 48], P('row', 'col'), may hold values 0 or 1
- target_bands: int32 [2, 16, 12, 1], P('row', 'col'), may hold values from 0 to 1; in each aligned block of 12 rows (0 to 11, 12 to 23, ..., all dimensions but the last counted through in order) at most 6 rows name the same one
Outputs:
- stochastic_result: bfloat16 [1024, 6144], P('row', 'col')
- redistributed_result: bfloat16 [3072, 2048], P('row', 'col')
The draws below stay inside these ranges and needn't reach their ends.
Inputs may be any that keep to these rules, and one draw needn't show every extreme that they name: `target_bands`: among the tiles of one block no destination is named more than 6 times, and in some block one destination is named exactly 6 times.
All inputs are finite; a program needn't handle non-finite values. No bound on the sum of `first_factor_support` or of `second_factor_support` or of `retained_blocks` on one device may be relied on, other than what follows from the above.
Results may differ from the reference program's by a relative error of at most 0.001.
Values may be sent and summed in bfloat16 or wider, within the bound.
No kernel may reach another device: no remote copies, remote signals or barrier semaphores. Data moves between devices by JAX's collectives and lax.ppermute only.
A program may use at most 64 MiB of HBM per device.

```python
import math
import jax
import jax.numpy as jnp
import numpy as np

BLOCK_EDGE = 128
BLOCK_LINES = 4
BLOCK_VERTICALS = 3
KT = 1
HORIZONTAL_BANDS = 2
VERTICAL_BANDS = 16
NR = 1024
NC = 6144
K = 2048
BERTH_LIMIT = 6


def draw_first_factor_strip(key, part):
    first, second = jax.random.split(key)
    ramp = (3.0 ** (jnp.arange(NR).astype(jnp.float32) / max(NR - 1, 1)))[:, None]
    base = jnp.clip(jax.random.normal(first, (NR, K), jnp.float32), -5.0, 5.0)
    rough = jnp.exp(jax.random.uniform(second, (NR, 1), jnp.float32, 0.0, math.log(3.0)))
    return (base * ramp * rough / 3.0).astype(jnp.bfloat16)


def touch_ends(values, own_key, smallest, largest):
    longest = values.shape.index(max(values.shape))
    spots = []
    for shift in (0, 1):
        where = [jax.random.randint(jax.random.fold_in(own_key, axis), (), 0, length) for axis, length in enumerate(values.shape)]
        where[longest] = (where[longest] + shift) % values.shape[longest]
        spots.append(tuple(where))
    return values.at[spots[0]].set(smallest).at[spots[1]].set(largest)


def levels(own_key, dims, cuts, least, high):
    factor_of = 1.0
    for dim, parts in cuts:
        heights = jax.random.uniform(jax.random.fold_in(jax.random.fold_in(own_key, 6), dim), (parts,), jnp.float32, least / len(cuts), high / len(cuts))
        factor_of = factor_of * jnp.repeat(jnp.exp(heights), dims[dim] // parts).reshape((-1,) + (1,) * (len(dims) - 1 - dim))
    return factor_of


def deal_out(key, own, number, rows, number_of, top, reach, skew):
    order = jax.random.permutation(key, number_of)
    packed, usual = shares(number_of, rows * top, reach, skew, True), shares(number_of, rows * top, reach, skew, False)
    places = jnp.arange(number_of)

    def named(sizes, offset_by):
        used = int((sizes > 0).sum())
        fixed = max(1, used // 4)
        passed = fixed + (places - fixed + offset_by * (used - fixed)) % max(1, number_of - fixed)
        return jnp.zeros((number_of,), jnp.int32).at[order[jnp.where(places < fixed, places, passed)]].set(jnp.asarray(sizes, jnp.int32))

    sizes = jnp.where(number % 4 == 0, named(packed, number // 4), named(usual, number - number // 4 - 1))
    mixed = jax.random.permutation(jax.random.fold_in(own, 3), number_of)
    donor, taker = mixed[0:number_of // 2 * 2:2], mixed[1:number_of // 2 * 2:2]
    margin = jnp.minimum(sizes[donor] - 1, reach - sizes[taker]) // 2
    margin = jnp.where((donor == order[0]) | (taker == order[0]) | (sizes[taker] == 0), 0, jnp.maximum(margin, 0))
    passed = jax.random.randint(jax.random.fold_in(own, 4), (number_of // 2,), 0, 1 << 20) % (margin + 1)
    sizes = sizes.at[donor].add(-passed).at[taker].add(passed)
    items = jnp.searchsorted(jnp.cumsum(sizes), jnp.arange(rows * top), side="right").astype(jnp.int32)
    listing = items.reshape(top, rows).T
    listing = listing[jax.random.permutation(jax.random.fold_in(own, 1), rows)]
    offset_by = jax.random.randint(jax.random.fold_in(own, 2), (rows, 1), 0, top)
    return jnp.take_along_axis(listing, (jnp.arange(top)[None, :] + offset_by) % top, axis=1)


def shares(number_of, total, reach, lean, full):
    weights = [(1 << 20) // math.isqrt(rank ** lean) + 1 for rank in range(1, number_of + 1)]
    largest = reach if full else min(reach, max(-(-total // number_of), total * weights[0] // sum(weights)))
    least = 1 if total - largest >= number_of - 1 else 0
    holding, surplus = [largest] + [least] * (number_of - 1), total - largest - least * (number_of - 1)
    while surplus > 0:
        candidates = [i for i in range(1, number_of) if holding[i] < largest] or [i for i in range(1, number_of) if holding[i] < reach]
        mass, budget = sum([weights[i] for i in candidates]), surplus
        for i in candidates:
            more = min(reach - holding[i], max(1, budget * weights[i] // mass), surplus)
            holding[i] = holding[i] + more
            surplus = surplus - more
    return np.array(holding)


def noise(key, extent, scale, limit, shards=(), held_as=jnp.bfloat16):
    values = jax.random.normal(key, extent, jnp.float32) * scale
    if len(shards) > 0:
        values = levels(key, extent, shards, -0.22, 0.18) * values
    return jnp.clip(values, min=-limit, max=limit).astype(held_as)


def setup_inputs(seed: int = 0) -> dict:
    key_of = jax.random.split(jax.random.key(seed), 7)
    first_factor_strip = draw_first_factor_strip(jax.random.fold_in(key_of[6], 71), 0)
    second_factor_strip = noise(key_of[1], (K, NC), K ** -0.5, 0.125, ((0, 2), (1, 16)))
    first_factor_support = touch_ends((jax.random.randint(key_of[2], (BLOCK_LINES * HORIZONTAL_BANDS, KT * VERTICAL_BANDS), 0, 8) < 5).astype(jnp.int32), jax.random.fold_in(key_of[2], 1), 0, 1)
    second_factor_support = touch_ends((jax.random.randint(key_of[3], (KT * VERTICAL_BANDS, BLOCK_VERTICALS * VERTICAL_BANDS), 0, 8) < 5).astype(jnp.int32), jax.random.fold_in(key_of[3], 1), 0, 1)
    retained_blocks = touch_ends((jax.random.randint(key_of[4], (BLOCK_LINES * HORIZONTAL_BANDS, BLOCK_VERTICALS * VERTICAL_BANDS), 0, 8) < 7).astype(jnp.int32), jax.random.fold_in(key_of[4], 1), 0, 1)
    target_bands_keys = jax.random.split(jax.random.fold_in(key_of[5], 1), HORIZONTAL_BANDS * VERTICAL_BANDS * (BLOCK_LINES * BLOCK_VERTICALS) // (BLOCK_LINES * BLOCK_VERTICALS))
    target_bands_turns = jax.random.permutation(jax.random.fold_in(key_of[5], 3), HORIZONTAL_BANDS * VERTICAL_BANDS * (BLOCK_LINES * BLOCK_VERTICALS) // (BLOCK_LINES * BLOCK_VERTICALS))
    target_bands = jax.vmap(lambda own, number: deal_out(jax.random.fold_in(key_of[5], 2), own, number, BLOCK_LINES * BLOCK_VERTICALS, HORIZONTAL_BANDS, 1, BERTH_LIMIT, 2))(target_bands_keys, target_bands_turns).reshape((HORIZONTAL_BANDS, VERTICAL_BANDS, BLOCK_LINES * BLOCK_VERTICALS, 1))
    return {"first_factor_strip": first_factor_strip, "second_factor_strip": second_factor_strip, "first_factor_support": first_factor_support, "second_factor_support": second_factor_support, "retained_blocks": retained_blocks, "target_bands": target_bands}


def squaring_pass(values, pattern):
    row_tiles, col_tiles = pattern.shape
    shaped = values.reshape(row_tiles, BLOCK_EDGE, col_tiles, BLOCK_EDGE)
    return (shaped * pattern[:, None, :, None].astype(values.dtype)).reshape(values.shape)


def reference(first_factor_strip, second_factor_strip, first_factor_support, second_factor_support, retained_blocks, target_bands):
    a_eff = squaring_pass(first_factor_strip, first_factor_support)
    b_eff = squaring_pass(second_factor_strip, second_factor_support)
    multiplied_blocks = jnp.dot(a_eff, b_eff, preferred_element_type=jnp.float32)
    powered_blocks = squaring_pass(multiplied_blocks * multiplied_blocks, retained_blocks)
    col_mean = jnp.sum(powered_blocks, axis=0) / NR
    stochastic_result = (powered_blocks / (col_mean + 1e-5)).astype(jnp.bfloat16)
    tile_count = BLOCK_LINES * BLOCK_VERTICALS
    tile_stack = stochastic_result.reshape(HORIZONTAL_BANDS, BLOCK_LINES, BLOCK_EDGE, VERTICAL_BANDS, BLOCK_VERTICALS, BLOCK_EDGE)
    tile_stack = tile_stack.transpose(0, 3, 1, 4, 2, 5).reshape(HORIZONTAL_BANDS, VERTICAL_BANDS, tile_count, BLOCK_EDGE, BLOCK_EDGE)
    targets = target_bands[..., 0]
    same_target = targets[..., :, None] == targets[..., None, :]
    earlier = jnp.arange(tile_count)[None, :] < jnp.arange(tile_count)[:, None]
    slot_rank = jnp.sum((same_target & earlier).astype(jnp.int32), axis=-1).astype(jnp.int32)
    position = targets * BERTH_LIMIT + slot_rank
    selector = (position[..., None] == jnp.arange(HORIZONTAL_BANDS * BERTH_LIMIT)[None, None, None, :]).astype(jnp.float32)
    selector = selector.reshape(HORIZONTAL_BANDS, VERTICAL_BANDS, tile_count, HORIZONTAL_BANDS, BERTH_LIMIT)
    positioned_blocks = jnp.einsum('ijtds,ijtab->disajb', selector, tile_stack.astype(jnp.float32))
    redistributed_result = positioned_blocks.reshape(HORIZONTAL_BANDS * HORIZONTAL_BANDS * BERTH_LIMIT * BLOCK_EDGE, VERTICAL_BANDS * BLOCK_EDGE).astype(jnp.bfloat16)
    return stochastic_result, redistributed_result
```

```python
import functools

import jax
import jax.numpy as jnp
from jax import lax
from jax.experimental import pallas as pl
from jax.experimental.pallas import tpu as pltpu
from jax.sharding import PartitionSpec as P

EDGE = 128
VMEM = pltpu.VMEM
SMEM = pltpu.SMEM
LIMIT = 48 * 1024 * 1024


def squaring_pass(values, pattern):
    row_tiles, col_tiles = pattern.shape
    shaped = values.reshape(row_tiles, EDGE, col_tiles, EDGE)
    return (shaped * pattern[:, None, :, None].astype(values.dtype)).reshape(values.shape)


def berths(tile_count, bands):
    return max(2, (tile_count + bands - 1) // bands)


def body_any(a, b, a_support, b_support, retained, target_bands):
    a_whole = lax.all_gather(squaring_pass(a, a_support), "col", axis=1, tiled=True)
    b_whole = lax.all_gather(squaring_pass(b, b_support), "row", axis=0, tiled=True)
    product = jnp.dot(a_whole, b_whole, preferred_element_type=jnp.float32)
    inflated = squaring_pass(product * product, retained)
    totals = lax.psum(jnp.sum(inflated, axis=0), "row")
    bands = lax.axis_size("row")
    all_rows = inflated.shape[0] * bands
    result = (inflated / (totals / all_rows + 1e-05)).astype(jnp.bfloat16)
    tile_rows, tile_cols = retained.shape
    tile_count = tile_rows * tile_cols
    limit = berths(tile_count, bands)
    stack = result.reshape(tile_rows, EDGE, tile_cols, EDGE).transpose(0, 2, 1, 3)
    stack = stack.reshape(tile_count, EDGE * EDGE)
    targets = target_bands.reshape(tile_count)
    same_target = targets[:, None] == targets[None, :]
    earlier = jnp.arange(tile_count)[None, :] < jnp.arange(tile_count)[:, None]
    rank = jnp.sum((same_target & earlier).astype(jnp.int32), axis=1)
    position = targets * limit + rank
    selector = (jnp.arange(bands * limit)[:, None] == position[None, :]).astype(jnp.bfloat16)
    outgoing = jnp.dot(selector, stack, preferred_element_type=jnp.float32).astype(jnp.bfloat16)
    outgoing = outgoing.reshape(bands, limit, EDGE, EDGE)
    delivered = lax.all_to_all(outgoing, "row", split_axis=0, concat_axis=0, tiled=True)
    return result, delivered.reshape(bands * limit * EDGE, EDGE)


def mask_kernel(support, a, out):
    for r in range(support.shape[0]):
        rows = pl.ds(r * EDGE, EDGE)
        out[rows, :] = a[rows, :] * support[r].astype(jnp.float32).astype(a.dtype)


def product_kernel(where, own_support, other_support, retained, b_own, b_other, *refs):
    *pieces, inflated, totals, b_scratch = refs
    tiles = b_own.shape[0] // EDGE
    cols = b_own.shape[1] // EDGE
    i, j = where[0], where[1]
    for half, support, b in ((i, own_support, b_own), (1 - i, other_support, b_other)):
        for q in range(tiles):
            m = lax.bitwise_xor(j, half * tiles + q)
            for c in range(cols):
                lanes = pl.ds(c * EDGE, EDGE)
                keep = support[q * cols + c].astype(jnp.float32).astype(b.dtype)
                b_scratch[m, :, lanes] = b[q * EDGE:(q + 1) * EDGE, lanes] * keep
    a = jnp.concatenate([p[...] for p in pieces], axis=1)
    b = b_scratch[...].reshape(-1, b_own.shape[1])
    product = jnp.dot(a, b, preferred_element_type=jnp.float32)
    squares = product * product
    rows = a.shape[0] // EDGE
    total = [None] * cols
    for r in range(rows):
        for c in range(cols):
            keep = retained[r * cols + c].astype(jnp.float32)
            tile = squares[r * EDGE:(r + 1) * EDGE, c * EDGE:(c + 1) * EDGE] * keep
            inflated[pl.ds(r * EDGE, EDGE), pl.ds(c * EDGE, EDGE)] = tile
            part = jnp.sum(tile.reshape(EDGE // 8, 8, EDGE), axis=0)
            total[c] = part if r == 0 else total[c] + part
    for c in range(cols):
        totals[:, pl.ds(c * EDGE, EDGE)] = total[c]


def finish_kernel(all_rows, limit, where, targets, inflated, own, other, result, placed, outgoing):
    cols = inflated.shape[1] // EDGE
    rows = inflated.shape[0] // EDGE
    i = where[0]
    total = jnp.sum(own[...] + other[...], axis=0, keepdims=True)
    scale = 1.0 / (total / all_rows + 1e-05)
    if 2 * limit != rows * cols:
        placed[...] = jnp.zeros_like(placed)
        outgoing[...] = jnp.zeros_like(outgoing)
    kept = jnp.int32(0)
    sent = jnp.int32(0)
    for t in range(rows * cols):
        r, c = t // cols, t % cols
        lanes = slice(c * EDGE, (c + 1) * EDGE)
        tile = inflated[r * EDGE:(r + 1) * EDGE, lanes] * scale[:, lanes]
        tile = tile.astype(jnp.bfloat16)
        result[r * EDGE:(r + 1) * EDGE, lanes] = tile
        stays = targets[t] == i

        @pl.when(stays)
        def _():
            placed[i * limit + kept] = tile

        @pl.when(jnp.logical_not(stays))
        def _():
            outgoing[sent] = tile

        one = stays.astype(jnp.int32)
        kept = kept + one
        sent = sent + 1 - one


def body_pair(a, b, a_support, b_support, retained, target_bands):
    n_col = lax.axis_size("col")
    swap = [(0, 1), (1, 0)]
    i, j = lax.axis_index("row"), lax.axis_index("col")
    where = jnp.stack([i, j]).astype(jnp.int32)

    def across(values, mask):
        return lax.ppermute(values, "col", [(k, k ^ mask) for k in range(n_col)])

    b_other = lax.ppermute(b, "row", swap)
    own_support = b_support.reshape(-1)
    other_support = lax.ppermute(b_support, "row", swap).reshape(-1)
    whole = pl.BlockSpec(memory_space=VMEM)
    scalars = pl.BlockSpec(memory_space=SMEM)
    a_eff = pl.pallas_call(
        mask_kernel,
        out_shape=jax.ShapeDtypeStruct(a.shape, a.dtype),
        in_specs=[scalars, whole],
        out_specs=whole,
        name="mask_left",
    )(a_support.reshape(-1), a)

    pieces = {0: a_eff}
    bits = [k for k in (1 << e for e in range(n_col.bit_length())) if 2 < k < n_col]
    for bit in reversed(bits):
        pieces[bit] = across(a_eff, bit)
    pieces[2] = across(a_eff, 2)
    for m in range(4, n_col, 4):
        if m not in pieces:
            low = m & -m
            pieces[m] = across(pieces[m ^ low], low)
    for m in range(4, n_col, 4):
        pieces[m | 2] = across(pieces[m], 2)
    order = sorted(pieces)
    for m in order:
        pieces[m | 1] = across(pieces[m], 1)
    stacked = [pieces[m] for m in range(n_col)]

    rows, columns = a.shape[0], b.shape[1]
    inflated, totals = pl.pallas_call(
        product_kernel,
        out_shape=(
            jax.ShapeDtypeStruct((rows, columns), jnp.float32),
            jax.ShapeDtypeStruct((8, columns), jnp.float32),
        ),
        in_specs=[scalars] * 4 + [whole] * (2 + n_col),
        out_specs=(whole, whole),
        scratch_shapes=[VMEM((n_col, EDGE, columns), b.dtype)],
        compiler_params=pltpu.CompilerParams(vmem_limit_bytes=LIMIT),
        name="expand_inflate",
    )(where, own_support, other_support, retained.reshape(-1), b, b_other, *stacked)

    other_totals = lax.ppermute(totals, "row", swap)
    tile_count = retained.shape[0] * retained.shape[1]
    limit = berths(tile_count, 2)
    result, placed, outgoing = pl.pallas_call(
        functools.partial(finish_kernel, 2 * rows, limit),
        out_shape=(
            jax.ShapeDtypeStruct((rows, columns), jnp.bfloat16),
            jax.ShapeDtypeStruct((2 * limit, EDGE, EDGE), jnp.bfloat16),
            jax.ShapeDtypeStruct((limit, EDGE, EDGE), jnp.bfloat16),
        ),
        in_specs=[scalars] * 2 + [whole] * 3,
        out_specs=(whole, whole, whole),
        compiler_params=pltpu.CompilerParams(vmem_limit_bytes=LIMIT),
        name="normalise_place",
    )(where, target_bands.reshape(-1), inflated, totals, other_totals)
    arrived = lax.ppermute(outgoing, "row", swap)
    placed = lax.dynamic_update_slice(placed, arrived, ((1 - i) * limit, 0, 0))
    return result, placed.reshape(2 * limit * EDGE, EDGE)


def solution(mesh):
    n_row, n_col = mesh.shape["row"], mesh.shape["col"]
    paired = n_row == 2 and n_col >= 4 and n_col & (n_col - 1) == 0
    placed = (P("row", "col"),) * 5 + (P("row", "col", None, None),)
    return jax.shard_map(
        body_pair if paired else body_any,
        mesh=mesh,
        in_specs=placed,
        out_specs=(P("row", "col"), P("row", "col")),
        check_vma=False,
    )
```

```python
import functools

import jax
import jax.numpy as jnp
from jax import lax
from jax.experimental import pallas as pl
from jax.experimental.pallas import tpu as pltpu
from jax.sharding import PartitionSpec as P

EDGE = 128
VMEM = pltpu.VMEM
SMEM = pltpu.SMEM
LIMIT = 48 * 1024 * 1024
STEPS = 65535.0
HALF = 32768
TINY = 1e-23


def squaring_pass(values, pattern):
    row_tiles, col_tiles = pattern.shape
    shaped = values.reshape(row_tiles, EDGE, col_tiles, EDGE)
    return (shaped * pattern[:, None, :, None].astype(values.dtype)).reshape(values.shape)


def berths(tile_count, bands):
    return max(2, (tile_count + bands - 1) // bands)


def body_any(a, b, a_support, b_support, retained, target_bands):
    a_whole = lax.all_gather(squaring_pass(a, a_support), "col", axis=1, tiled=True)
    b_whole = lax.all_gather(squaring_pass(b, b_support), "row", axis=0, tiled=True)
    product = jnp.dot(a_whole, b_whole, preferred_element_type=jnp.float32)
    inflated = squaring_pass(product * product, retained)
    totals = lax.psum(jnp.sum(inflated, axis=0), "row")
    bands = lax.axis_size("row")
    all_rows = inflated.shape[0] * bands
    result = (inflated / (totals / all_rows + 1e-05)).astype(jnp.bfloat16)
    tile_rows, tile_cols = retained.shape
    tile_count = tile_rows * tile_cols
    limit = berths(tile_count, bands)
    stack = result.reshape(tile_rows, EDGE, tile_cols, EDGE).transpose(0, 2, 1, 3)
    stack = stack.reshape(tile_count, EDGE * EDGE)
    targets = target_bands.reshape(tile_count)
    same_target = targets[:, None] == targets[None, :]
    earlier = jnp.arange(tile_count)[None, :] < jnp.arange(tile_count)[:, None]
    rank = jnp.sum((same_target & earlier).astype(jnp.int32), axis=1)
    position = targets * limit + rank
    selector = (jnp.arange(bands * limit)[:, None] == position[None, :]).astype(jnp.bfloat16)
    outgoing = jnp.dot(selector, stack, preferred_element_type=jnp.float32).astype(jnp.bfloat16)
    outgoing = outgoing.reshape(bands, limit, EDGE, EDGE)
    delivered = lax.all_to_all(outgoing, "row", split_axis=0, concat_axis=0, tiled=True)
    return result, delivered.reshape(bands * limit * EDGE, EDGE)


def gather_product_kernel(mine, theirs, b_own, b_other, *refs):
    *pieces, product, b_last, b_scratch, b_local, sem = refs
    copy = pltpu.make_async_copy(b_own, b_local, sem)
    copy.start()
    tiles = b_local.shape[0] // EDGE
    cols = b_local.shape[1] // EDGE
    i, j = mine[0], mine[1]
    for half, support, b in ((1 - i, theirs, b_other), (i, mine, b_local)):
        if b is b_local:
            copy.wait()
        for q in range(tiles):
            m = lax.bitwise_xor(j, half * tiles + q)
            for c in range(cols):
                lanes = pl.ds(c * EDGE, EDGE)
                keep = support[2 + q * cols + c].astype(jnp.float32).astype(b.dtype)
                b_scratch[m, :, lanes] = b[q * EDGE:(q + 1) * EDGE, lanes] * keep
    n = len(pieces)
    a = jnp.concatenate([p[...] for p in pieces], axis=1)
    b = b_scratch[:n].reshape(n * EDGE, -1)
    product[...] = jnp.dot(a, b, preferred_element_type=jnp.float32)
    b_last[...] = b_scratch[n:].reshape(b_last.shape)


def inflate_kernel(offsets, mine, part, b_last, even, odd, product, stats, codes):
    retained, targets = offsets
    a = jnp.concatenate([even[...], odd[...]], axis=1)
    whole = part[...] + jnp.dot(a, b_last[...], preferred_element_type=jnp.float32)
    rows, cols = whole.shape[0] // EDGE, whole.shape[1] // EDGE
    tops = []
    for c in range(cols):
        lanes = pl.ds(c * EDGE, EDGE)
        total = top = None
        for r in range(rows):
            keep = mine[retained + r * cols + c].astype(jnp.float32)
            tile = jnp.abs(whole[r * EDGE:(r + 1) * EDGE, c * EDGE:(c + 1) * EDGE]) * keep
            product[pl.ds(r * EDGE, EDGE), lanes] = tile
            stacked = tile.reshape(EDGE // 8, 8, EDGE)
            sums, peak = jnp.sum(stacked * stacked, axis=0), jnp.max(stacked, axis=0)
            total = sums if r == 0 else total + sums
            top = peak if r == 0 else jnp.maximum(top, peak)
        stats[pl.ds(0, 8), lanes] = total
        stats[pl.ds(8, 8), lanes] = top
        top = jnp.max(top, axis=0, keepdims=True)
        tops.append(jnp.where(top > TINY, STEPS / jnp.maximum(top, TINY), 0.0))
    if codes.shape[0] * 2 != rows * cols:
        codes[...] = jnp.full_like(codes, -HALF)
    sent = jnp.int32(0)
    for t in range(rows * cols):
        r, c = t // cols, t % cols
        leaves = mine[targets + t] != mine[0]

        @pl.when(leaves)
        def _():
            tile = product[pl.ds(r * EDGE, EDGE), pl.ds(c * EDGE, EDGE)]
            steps = (tile * tops[c] + 0.5).astype(jnp.int32) - HALF
            codes[sent] = steps.astype(codes.dtype)

        sent = sent + leaves.astype(jnp.int32)


def finish_kernel(all_rows, targets, limit, mine, theirs, product, own, other, result, placed, step, scale):
    rows, cols = product.shape[0] // EDGE, product.shape[1] // EDGE
    i = mine[0]
    total = jnp.sum(own[0:8, :] + other[0:8, :], axis=0, keepdims=True)
    inverse = 1.0 / (total / all_rows + 1e-05)
    top = jnp.max(other[8:16, :], axis=0, keepdims=True) / STEPS
    if 2 * limit != rows * cols:
        placed[...] = jnp.zeros_like(placed)
        step[...] = jnp.zeros_like(step)
        scale[...] = jnp.zeros_like(scale)
    kept = jnp.int32(0)
    come = jnp.int32(0)
    for t in range(rows * cols):
        r, c = t // cols, t % cols
        lanes = slice(c * EDGE, (c + 1) * EDGE)
        tile = product[r * EDGE:(r + 1) * EDGE, lanes]
        tile = (tile * tile * inverse[:, lanes]).astype(result.dtype)
        result[r * EDGE:(r + 1) * EDGE, lanes] = tile
        stays = mine[targets + t] == i
        comes = theirs[targets + t] == i

        @pl.when(stays)
        def _():
            placed[i * limit + kept] = tile

        @pl.when(comes)
        def _():
            step[come] = top[:, lanes]
            scale[come] = inverse[:, lanes]

        kept = kept + stays.astype(jnp.int32)
        come = come + comes.astype(jnp.int32)


def body_pair(a, b, a_support, b_support, retained, target_bands):
    n_col = lax.axis_size("col")
    swap = [(0, 1), (1, 0)]
    i, j = lax.axis_index("row"), lax.axis_index("col")
    rows, columns = a.shape[0], b.shape[1]
    tile_count = retained.shape[0] * retained.shape[1]
    limit = berths(tile_count, 2)
    retained_at = 2 + b_support.size
    targets_at = retained_at + tile_count

    def across(values, mask):
        return lax.ppermute(values, "col", [(k, k ^ mask) for k in range(n_col)])

    b_other = lax.ppermute(b, "row", swap)
    a_eff = squaring_pass(a, a_support)
    high = n_col // 2
    pieces = {0: a_eff}
    bits = [1 << e for e in range(n_col.bit_length()) if 2 < 1 << e < n_col]
    for bit in reversed(bits):
        pieces[bit] = across(a_eff, bit)
    pieces[2] = across(a_eff, 2)
    for m in range(4, n_col, 4):
        if m not in pieces:
            low = m & -m
            pieces[m] = across(pieces[m ^ low], low)
    for m in range(4, n_col, 4):
        pieces[m | 2] = across(pieces[m], 2)
    for m in sorted(pieces):
        pieces[m | 1] = across(pieces[m], 1)
    pieces = [pieces[m] for m in range(n_col)]

    mine = jnp.concatenate(
        [
            jnp.stack([i, j]).astype(jnp.int32),
            b_support.reshape(-1),
            retained.reshape(-1),
            target_bands.reshape(-1),
        ]
    )
    late, _ = lax.optimization_barrier((mine, pieces[high]))
    theirs = lax.ppermute(late, "row", swap)

    whole = pl.BlockSpec(memory_space=VMEM)
    scalars = pl.BlockSpec(memory_space=SMEM)
    params = pltpu.CompilerParams(vmem_limit_bytes=LIMIT)
    part, b_last = pl.pallas_call(
        gather_product_kernel,
        out_shape=(
            jax.ShapeDtypeStruct((rows, columns), jnp.float32),
            jax.ShapeDtypeStruct((2 * EDGE, columns), b.dtype),
        ),
        in_specs=[scalars] * 2 + [pl.BlockSpec(memory_space=pl.ANY)] + [whole] * (n_col - 1),
        out_specs=(whole, whole),
        scratch_shapes=[
            VMEM((n_col, EDGE, columns), b.dtype),
            VMEM(b.shape, b.dtype),
            pltpu.SemaphoreType.DMA,
        ],
        compiler_params=params,
        name="gather_product",
    )(mine, theirs, b, b_other, *pieces[:-2])

    product, stats, codes = pl.pallas_call(
        functools.partial(inflate_kernel, (retained_at, targets_at)),
        out_shape=(
            jax.ShapeDtypeStruct((rows, columns), jnp.float32),
            jax.ShapeDtypeStruct((16, columns), jnp.float32),
            jax.ShapeDtypeStruct((limit, EDGE, EDGE), jnp.int16),
        ),
        in_specs=[scalars] + [whole] * 4,
        out_specs=(whole, whole, whole),
        compiler_params=params,
        name="inflate",
    )(mine, part, b_last, *pieces[-2:])

    other_stats = lax.ppermute(stats, "row", swap)
    arrived = lax.ppermute(codes, "row", swap)
    result, placed, step, scale = pl.pallas_call(
        functools.partial(finish_kernel, 2 * rows, targets_at, limit),
        out_shape=(
            jax.ShapeDtypeStruct((rows, columns), jnp.bfloat16),
            jax.ShapeDtypeStruct((2 * limit, EDGE, EDGE), jnp.bfloat16),
            jax.ShapeDtypeStruct((limit, 1, EDGE), jnp.float32),
            jax.ShapeDtypeStruct((limit, 1, EDGE), jnp.float32),
        ),
        in_specs=[scalars] * 2 + [whole] * 3,
        out_specs=(whole,) * 4,
        compiler_params=params,
        name="finish",
    )(mine, theirs, product, stats, other_stats)
    values = (arrived.astype(jnp.float32) + HALF) * step
    values = (values * values * scale).astype(jnp.bfloat16)
    placed = lax.dynamic_update_slice(placed, values, ((1 - i) * limit, 0, 0))
    return result, placed.reshape(2 * limit * EDGE, EDGE)


def solution(mesh):
    n_row, n_col = mesh.shape["row"], mesh.shape["col"]
    paired = n_row == 2 and n_col >= 4 and n_col & (n_col - 1) == 0
    placed = (P("row", "col"),) * 5 + (P("row", "col", None, None),)
    return jax.shard_map(
        body_pair if paired else body_any,
        mesh=mesh,
        in_specs=placed,
        out_specs=(P("row", "col"), P("row", "col")),
        check_vma=False,
    )
```

```python
import functools

import jax
import jax.numpy as jnp
from jax import lax
from jax.experimental import pallas as pl
from jax.experimental.pallas import tpu as pltpu
from jax.sharding import PartitionSpec as P

EDGE = 128
VMEM = pltpu.VMEM
SMEM = pltpu.SMEM
LIMIT = 48 * 1024 * 1024
STEPS = 65535.0
HALF = 32768
TINY = 1e-23
MASK_LIMIT = 60 * 1024 * 1024


def squaring_pass(values, pattern):
    row_tiles, col_tiles = pattern.shape
    shaped = values.reshape(row_tiles, EDGE, col_tiles, EDGE)
    return (shaped * pattern[:, None, :, None].astype(values.dtype)).reshape(values.shape)


def berths(tile_count, bands):
    return max(2, (tile_count + bands - 1) // bands)


def body_any(a, b, a_support, b_support, retained, target_bands):
    a_whole = lax.all_gather(squaring_pass(a, a_support), "col", axis=1, tiled=True)
    b_whole = lax.all_gather(squaring_pass(b, b_support), "row", axis=0, tiled=True)
    product = jnp.dot(a_whole, b_whole, preferred_element_type=jnp.float32)
    inflated = squaring_pass(product * product, retained)
    totals = lax.psum(jnp.sum(inflated, axis=0), "row")
    bands = lax.axis_size("row")
    all_rows = inflated.shape[0] * bands
    result = (inflated / (totals / all_rows + 1e-05)).astype(jnp.bfloat16)
    tile_rows, tile_cols = retained.shape
    tile_count = tile_rows * tile_cols
    limit = berths(tile_count, bands)
    stack = result.reshape(tile_rows, EDGE, tile_cols, EDGE).transpose(0, 2, 1, 3)
    stack = stack.reshape(tile_count, EDGE * EDGE)
    targets = target_bands.reshape(tile_count)
    same_target = targets[:, None] == targets[None, :]
    earlier = jnp.arange(tile_count)[None, :] < jnp.arange(tile_count)[:, None]
    rank = jnp.sum((same_target & earlier).astype(jnp.int32), axis=1)
    position = targets * limit + rank
    selector = (jnp.arange(bands * limit)[:, None] == position[None, :]).astype(jnp.bfloat16)
    outgoing = jnp.dot(selector, stack, preferred_element_type=jnp.float32).astype(jnp.bfloat16)
    outgoing = outgoing.reshape(bands, limit, EDGE, EDGE)
    delivered = lax.all_to_all(outgoing, "row", split_axis=0, concat_axis=0, tiled=True)
    return result, delivered.reshape(bands * limit * EDGE, EDGE)


def mask_kernel(a_support, b_support, a, b, a_out, b_out, a_keep, b_keep, a_local, b_local, sems):
    rows, tiles, cols = a.shape[0] // EDGE, b.shape[0] // EDGE, b.shape[1] // EDGE
    copies = [
        pltpu.make_async_copy(source, local, sems.at[k])
        for k, (source, local) in enumerate(((a_support, a_keep), (b_support, b_keep), (a, a_local), (b, b_local)))
    ]
    for copy in copies:
        copy.start()
    copies[0].wait()
    copies[2].wait()
    for r in range(rows):
        band = slice(r * EDGE, (r + 1) * EDGE)
        a_out[band, :] = a_local[band, :] * a_keep[0, r].astype(jnp.float32).astype(a.dtype)
    copies[1].wait()
    copies[3].wait()
    for q in range(tiles):
        band = slice(q * EDGE, (q + 1) * EDGE)
        for c in range(cols):
            lanes = slice(c * EDGE, (c + 1) * EDGE)
            b_out[band, lanes] = b_local[band, lanes] * b_keep[c, q].astype(jnp.float32).astype(b.dtype)


def gather_product_kernel(where, retained, targets, b_own, b_other, *refs):
    *pieces, product, b_last, ints, b_scratch = refs
    tiles = b_own.shape[0] // EDGE
    cols = b_own.shape[1] // EDGE
    rows = product.shape[0] // EDGE
    n = len(pieces)
    i, j = where[0], where[1]
    ints[0] = i
    for r in range(rows):
        for c in range(cols):
            ints[1 + r * cols + c] = retained[r, c]
            ints[1 + rows * cols + r * cols + c] = targets[0, r * cols + c]
    for half, b in ((i, b_own), (1 - i, b_other)):
        for q in range(tiles):
            m = lax.bitwise_xor(j, half * tiles + q)
            b_scratch[m] = b[q * EDGE:(q + 1) * EDGE, :]
    b = b_scratch[:n].reshape(n * EDGE, -1)
    a = jnp.concatenate([p[...] for p in pieces], axis=1)
    product[...] = jnp.dot(a, b, preferred_element_type=jnp.float32)
    b_last[...] = b_scratch[n:].reshape(b_last.shape)


def inflate_kernel(ints, part, b_last, even, odd, product, stats, codes):
    rows, cols = part.shape[0] // EDGE, part.shape[1] // EDGE
    count = rows * cols
    a = jnp.concatenate([even[...], odd[...]], axis=1)
    whole = part[...] + jnp.dot(a, b_last[...], preferred_element_type=jnp.float32)
    tops = []
    for c in range(cols):
        lanes = pl.ds(c * EDGE, EDGE)
        total = top = None
        for r in range(rows):
            keep = ints[1 + r * cols + c].astype(jnp.float32)
            tile = jnp.abs(whole[r * EDGE:(r + 1) * EDGE, c * EDGE:(c + 1) * EDGE]) * keep
            product[pl.ds(r * EDGE, EDGE), lanes] = tile
            stacked = tile.reshape(EDGE // 8, 8, EDGE)
            sums, peak = jnp.sum(stacked * stacked, axis=0), jnp.max(stacked, axis=0)
            total = sums if r == 0 else total + sums
            top = peak if r == 0 else jnp.maximum(top, peak)
        stats[pl.ds(0, 8), lanes] = total
        stats[pl.ds(8, 8), lanes] = top
        top = jnp.max(top, axis=0, keepdims=True)
        tops.append(jnp.where(top > TINY, STEPS / jnp.maximum(top, TINY), 0.0))
    if codes.shape[0] * 2 != count:
        codes[...] = jnp.full_like(codes, -HALF)
        stats[pl.ds(16, stats.shape[0] - 16), :] = jnp.zeros((stats.shape[0] - 16, cols * EDGE), jnp.float32)
    column = lax.broadcasted_iota(jnp.int32, (1, cols * EDGE), 1) // EDGE
    sent = jnp.int32(0)
    for t in range(count):
        r, c = t // cols, t % cols
        leaves = ints[1 + count + t] != ints[0]

        @pl.when(leaves)
        def _():
            tile = product[pl.ds(r * EDGE, EDGE), pl.ds(c * EDGE, EDGE)]
            steps = (tile * tops[c] + 0.5).astype(jnp.int32) - HALF
            codes[sent] = steps.astype(codes.dtype)
            stats[pl.ds(16 + sent, 1), :] = (column == c).astype(jnp.float32)

        sent = sent + leaves.astype(jnp.int32)


def finish_kernel(all_rows, limit, ints, product, own, other, result, placed, step, scale):
    rows, cols = product.shape[0] // EDGE, product.shape[1] // EDGE
    i = ints[0]
    total = jnp.sum(own[0:8, :] + other[0:8, :], axis=0, keepdims=True)
    inverse = 1.0 / (total / all_rows + 1e-05)
    top = jnp.max(other[8:16, :], axis=0, keepdims=True) / STEPS
    for s in range(limit):
        chosen = other[16 + s:17 + s, :]
        step[s] = sum((chosen * top)[:, c * EDGE:(c + 1) * EDGE] for c in range(cols))
        scale[s] = sum((chosen * inverse)[:, c * EDGE:(c + 1) * EDGE] for c in range(cols))
    if 2 * limit != rows * cols:
        placed[...] = jnp.zeros_like(placed)
    kept = jnp.int32(0)
    for t in range(rows * cols):
        r, c = t // cols, t % cols
        lanes = slice(c * EDGE, (c + 1) * EDGE)
        tile = product[r * EDGE:(r + 1) * EDGE, lanes]
        tile = (tile * tile * inverse[:, lanes]).astype(result.dtype)
        result[r * EDGE:(r + 1) * EDGE, lanes] = tile
        stays = ints[1 + rows * cols + t] == i

        @pl.when(stays)
        def _():
            placed[i * limit + kept] = tile

        kept = kept + stays.astype(jnp.int32)


def body_pair(a, b, a_support, b_support, retained, target_bands):
    n_col = lax.axis_size("col")
    swap = [(0, 1), (1, 0)]
    i, j = lax.axis_index("row"), lax.axis_index("col")
    rows, columns = a.shape[0], b.shape[1]
    tile_count = retained.shape[0] * retained.shape[1]
    limit = berths(tile_count, 2)

    def across(values, mask):
        return lax.ppermute(values, "col", [(k, k ^ mask) for k in range(n_col)])

    whole = pl.BlockSpec(memory_space=VMEM)
    scalars = pl.BlockSpec(memory_space=SMEM)
    params = pltpu.CompilerParams(vmem_limit_bytes=LIMIT)
    a_eff, b_eff = pl.pallas_call(
        mask_kernel,
        out_shape=(pltpu.VMEM(a.shape, a.dtype), pltpu.VMEM(b.shape, b.dtype)),
        in_specs=[pl.BlockSpec(memory_space=pltpu.HBM)] * 4,
        out_specs=(whole, whole),
        scratch_shapes=[
            SMEM(a_support.T.shape, jnp.int32),
            SMEM(b_support.T.shape, jnp.int32),
            VMEM(a.shape, a.dtype),
            VMEM(b.shape, b.dtype),
            pltpu.SemaphoreType.DMA((4,)),
        ],
        compiler_params=pltpu.CompilerParams(vmem_limit_bytes=MASK_LIMIT),
        name="mask_factors",
    )(a_support.T, b_support.T, a, b)
    b_other = lax.ppermute(b_eff, "row", swap)
    pieces = {0: a_eff}
    high = n_col // 2
    for m, base in ((8, 0), (4, 0), (2, 0), (12, 8), (10, 8), (6, 2), (14, 12)):
        pieces[m] = across(pieces[base], m ^ base)
    for m in sorted(pieces):
        if m != n_col - 2:
            pieces[m | 1] = across(pieces[m], 1)

    where = jnp.stack([i, j]).astype(jnp.int32)
    targets = target_bands.reshape(1, tile_count)
    first = n_col - 2
    part, b_last, ints = pl.pallas_call(
        gather_product_kernel,
        out_shape=(
            jax.ShapeDtypeStruct((rows, columns), jnp.float32),
            jax.ShapeDtypeStruct((2 * EDGE, columns), b.dtype),
            jax.ShapeDtypeStruct((1 + 2 * tile_count,), jnp.int32),
        ),
        in_specs=[scalars] * 3 + [whole] * (2 + first),
        out_specs=(whole, whole, scalars),
        scratch_shapes=[
            VMEM((n_col, EDGE, columns), b.dtype),
        ],
        compiler_params=params,
        cost_estimate=pl.CostEstimate(
            flops=2 * rows * columns * n_col * EDGE, bytes_accessed=8 * 1024 * 1024, transcendentals=0
        ),
        name="gather_product",
    )(where, retained, targets, b_eff, b_other, *[pieces[m] for m in range(first)])
    even, part = lax.optimization_barrier((pieces[first], part))
    odd = across(even, 1)

    product, stats, codes = pl.pallas_call(
        inflate_kernel,
        out_shape=(
            jax.ShapeDtypeStruct((rows, columns), jnp.float32),
            jax.ShapeDtypeStruct((16 + (limit + 7) // 8 * 8, columns), jnp.float32),
            jax.ShapeDtypeStruct((limit, EDGE, EDGE), jnp.int16),
        ),
        in_specs=[scalars] + [whole] * 4,
        out_specs=(whole, whole, whole),
        compiler_params=params,
        name="inflate",
    )(ints, part, b_last, even, odd)

    other_stats = lax.ppermute(stats, "row", swap)
    arrived = lax.ppermute(codes, "row", swap)
    result, placed, step, scale = pl.pallas_call(
        functools.partial(finish_kernel, 2 * rows, limit),
        out_shape=(
            jax.ShapeDtypeStruct((rows, columns), jnp.bfloat16),
            jax.ShapeDtypeStruct((2 * limit, EDGE, EDGE), jnp.bfloat16),
            jax.ShapeDtypeStruct((limit, 1, EDGE), jnp.float32),
            jax.ShapeDtypeStruct((limit, 1, EDGE), jnp.float32),
        ),
        in_specs=[scalars] + [whole] * 3,
        out_specs=(whole,) * 4,
        compiler_params=params,
        name="finish",
    )(ints, product, stats, other_stats)
    values = (arrived.astype(jnp.float32) + HALF) * step
    values = (values * values * scale).astype(jnp.bfloat16)
    placed = lax.dynamic_update_slice(placed, values, ((1 - i) * limit, 0, 0))
    return result, placed.reshape(2 * limit * EDGE, EDGE)


def solution(mesh):
    n_row, n_col = mesh.shape["row"], mesh.shape["col"]
    paired = n_row == 2 and n_col >= 16 and n_col & (n_col - 1) == 0
    placed = (P("row", "col"),) * 5 + (P("row", "col", None, None),)
    return jax.shard_map(
        body_pair if paired else body_any,
        mesh=mesh,
        in_specs=placed,
        out_specs=(P("row", "col"), P("row", "col")),
        check_vma=False,
    )
```

```python
import functools

import jax
import jax.numpy as jnp
from jax import lax
from jax.experimental import pallas as pl
from jax.experimental.pallas import tpu as pltpu
from jax.sharding import PartitionSpec as P

EDGE = 128
VMEM = pltpu.VMEM
SMEM = pltpu.SMEM
LIMIT = 48 * 1024 * 1024
STEPS = 65535.0
HALF = 32768
TINY = 1e-23
TIGHT = 60 * 1024 * 1024


def squaring_pass(values, pattern):
    row_tiles, col_tiles = pattern.shape
    shaped = values.reshape(row_tiles, EDGE, col_tiles, EDGE)
    return (shaped * pattern[:, None, :, None].astype(values.dtype)).reshape(values.shape)


def berths(tile_count, bands):
    return max(2, (tile_count + bands - 1) // bands)


def body_any(a, b, a_support, b_support, retained, target_bands):
    a_whole = lax.all_gather(squaring_pass(a, a_support), "col", axis=1, tiled=True)
    b_whole = lax.all_gather(squaring_pass(b, b_support), "row", axis=0, tiled=True)
    product = jnp.dot(a_whole, b_whole, preferred_element_type=jnp.float32)
    inflated = squaring_pass(product * product, retained)
    totals = lax.psum(jnp.sum(inflated, axis=0), "row")
    bands = lax.axis_size("row")
    all_rows = inflated.shape[0] * bands
    result = (inflated / (totals / all_rows + 1e-05)).astype(jnp.bfloat16)
    tile_rows, tile_cols = retained.shape
    tile_count = tile_rows * tile_cols
    limit = berths(tile_count, bands)
    stack = result.reshape(tile_rows, EDGE, tile_cols, EDGE).transpose(0, 2, 1, 3)
    stack = stack.reshape(tile_count, EDGE * EDGE)
    targets = target_bands.reshape(tile_count)
    same_target = targets[:, None] == targets[None, :]
    earlier = jnp.arange(tile_count)[None, :] < jnp.arange(tile_count)[:, None]
    rank = jnp.sum((same_target & earlier).astype(jnp.int32), axis=1)
    position = targets * limit + rank
    selector = (jnp.arange(bands * limit)[:, None] == position[None, :]).astype(jnp.bfloat16)
    outgoing = jnp.dot(selector, stack, preferred_element_type=jnp.float32).astype(jnp.bfloat16)
    outgoing = outgoing.reshape(bands, limit, EDGE, EDGE)
    delivered = lax.all_to_all(outgoing, "row", split_axis=0, concat_axis=0, tiled=True)
    return result, delivered.reshape(bands * limit * EDGE, EDGE)


def mask_kernel(a_support, b_support, retained, targets, a, b, a_out, b_out, ints, keeps, a_local, b_local, sems):
    a_keep, b_keep, retained_local, targets_local = keeps
    rows, tiles, cols = a.shape[0] // EDGE, b.shape[0] // EDGE, b.shape[1] // EDGE
    copies = [
        pltpu.make_async_copy(source, local, sems.at[k])
        for k, (source, local) in enumerate(
            (
                (a_support, a_keep),
                (b_support, b_keep),
                (a, a_local),
                (b, b_local),
                (retained, retained_local),
                (targets, targets_local),
            )
        )
    ]
    for copy in copies:
        copy.start()
    j = lax.axis_index("col")
    copies[0].wait()
    copies[2].wait()
    for r in range(rows):
        band = slice(r * EDGE, (r + 1) * EDGE)
        a_out[band, :] = a_local[band, :] * a_keep[0, r].astype(jnp.float32).astype(a.dtype)
    copies[1].wait()
    copies[3].wait()
    for q in range(tiles):
        band = slice(q * EDGE, (q + 1) * EDGE)
        place = lax.bitwise_and(lax.bitwise_xor(j, q), tiles - 1)
        for c in range(cols):
            lanes = slice(c * EDGE, (c + 1) * EDGE)
            keep = b_keep[c, q].astype(jnp.float32).astype(b.dtype)
            b_out[place, :, lanes] = b_local[band, lanes] * keep
    copies[4].wait()
    copies[5].wait()
    count = rows * cols
    lane = lax.broadcasted_iota(jnp.int32, ints.shape, 1)
    row = jnp.zeros(ints.shape, jnp.int32)
    for t in range(count):
        row = jnp.where(lane == t, retained_local[t // cols, t % cols], row)
        row = jnp.where(lane == count + t, targets_local[0, t], row)
    ints[...] = row


def side_by_side(pieces, groups, rows):
    shards = {
        m: piece[k * rows:(k + 1) * rows, :] for piece, group in zip(pieces, groups) for k, m in enumerate(group)
    }
    return jnp.concatenate([shards[m] for m in sorted(shards)], axis=1)


def gather_product_kernel(groups, late, b_own, b_other, *refs):
    *pieces, product, b_late = refs
    tiles, _, columns = b_own.shape
    own_first = lax.axis_index("col") // tiles == lax.axis_index("row")
    for first, second, chosen in ((b_own, b_other, own_first), (b_other, b_own, jnp.logical_not(own_first))):

        @pl.when(chosen)
        def _():
            a = side_by_side(pieces, groups, product.shape[0])
            low, high = late[0] - tiles, late[-1] + 1 - tiles
            b = jnp.concatenate([first[...], second[:low], second[high:]], axis=0)
            product[...] = jnp.dot(a, b.reshape(a.shape[1], columns), preferred_element_type=jnp.float32)
            b_late[...] = second[low:high].reshape(b_late.shape)


def inflate_kernel(groups, ints_far, part, b_late, *refs):
    *pieces, product, stats, codes, ints, sem = refs
    lookup = pltpu.make_async_copy(ints_far, ints, sem)
    lookup.start()
    i = lax.axis_index("row")
    rows, cols = part.shape[0] // EDGE, part.shape[1] // EDGE
    count = rows * cols
    a = side_by_side(pieces, groups, part.shape[0])
    whole = part[...] + jnp.dot(a, b_late[...], preferred_element_type=jnp.float32)
    lookup.wait()
    tops = []
    for c in range(cols):
        lanes = pl.ds(c * EDGE, EDGE)
        total = top = None
        for r in range(rows):
            keep = ints[0, r * cols + c].astype(jnp.float32)
            tile = jnp.abs(whole[r * EDGE:(r + 1) * EDGE, c * EDGE:(c + 1) * EDGE]) * keep
            product[pl.ds(r * EDGE, EDGE), lanes] = tile
            stacked = tile.reshape(EDGE // 8, 8, EDGE)
            sums, peak = jnp.sum(stacked * stacked, axis=0), jnp.max(stacked, axis=0)
            total = sums if r == 0 else total + sums
            top = peak if r == 0 else jnp.maximum(top, peak)
        top = jnp.max(top, axis=0, keepdims=True)
        stats[pl.ds(0, 1), lanes] = jnp.sum(total, axis=0, keepdims=True)
        stats[pl.ds(1, 1), lanes] = top
        tops.append(jnp.where(top > TINY, STEPS / jnp.maximum(top, TINY), 0.0))
    if codes.shape[0] * 2 != count:
        codes[...] = jnp.full_like(codes, -HALF)
        stats[pl.ds(2, codes.shape[0]), :] = jnp.zeros((codes.shape[0], cols * EDGE), jnp.float32)
    column = lax.broadcasted_iota(jnp.int32, (1, cols * EDGE), 1) // EDGE
    sent = jnp.int32(0)
    for t in range(count):
        r, c = t // cols, t % cols
        leaves = ints[0, count + t] != i

        @pl.when(leaves)
        def _():
            tile = product[pl.ds(r * EDGE, EDGE), pl.ds(c * EDGE, EDGE)]
            steps = (tile * tops[c] + 0.5).astype(jnp.int32) - HALF
            codes[sent] = steps.astype(codes.dtype)
            stats[pl.ds(2 + sent, 1), :] = (column == c).astype(jnp.float32)

        sent = sent + leaves.astype(jnp.int32)


def finish_kernel(all_rows, limit, ints, product, own, other, result, placed, step, scale):
    rows, cols = product.shape[0] // EDGE, product.shape[1] // EDGE
    i = lax.axis_index("row")
    total = own[0:1, :] + other[0:1, :]
    inverse = 1.0 / (total / all_rows + 1e-05)
    top = other[1:2, :] / STEPS
    for s in range(limit):
        chosen = other[2 + s:3 + s, :]
        step[s] = sum((chosen * top)[:, c * EDGE:(c + 1) * EDGE] for c in range(cols))
        scale[s] = sum((chosen * inverse)[:, c * EDGE:(c + 1) * EDGE] for c in range(cols))
    if 2 * limit != rows * cols:
        placed[...] = jnp.zeros_like(placed)
    kept = jnp.int32(0)
    for t in range(rows * cols):
        r, c = t // cols, t % cols
        lanes = slice(c * EDGE, (c + 1) * EDGE)
        tile = product[r * EDGE:(r + 1) * EDGE, lanes]
        tile = (tile * tile * inverse[:, lanes]).astype(result.dtype)
        result[r * EDGE:(r + 1) * EDGE, lanes] = tile
        stays = ints[0, rows * cols + t] == i

        @pl.when(stays)
        def _():
            placed[i * limit + kept] = tile

        kept = kept + stays.astype(jnp.int32)


def body_pair(a, b, a_support, b_support, retained, target_bands):
    n_col = lax.axis_size("col")
    swap = [(0, 1), (1, 0)]
    i = lax.axis_index("row")
    rows, columns = a.shape[0], b.shape[1]
    tile_count = retained.shape[0] * retained.shape[1]
    limit = berths(tile_count, 2)

    def across(values, mask):
        return lax.ppermute(values, "col", [(k, k ^ mask) for k in range(n_col)])

    whole = pl.BlockSpec(memory_space=VMEM)
    scalars = pl.BlockSpec(memory_space=SMEM)
    params = pltpu.CompilerParams(vmem_limit_bytes=LIMIT)
    targets = target_bands.reshape(1, tile_count)
    a_eff, b_eff, ints = pl.pallas_call(
        mask_kernel,
        out_shape=(
            pltpu.VMEM(a.shape, a.dtype),
            pltpu.VMEM((b.shape[0] // EDGE, EDGE, columns), b.dtype),
            pltpu.VMEM((1, (2 * tile_count + EDGE - 1) // EDGE * EDGE), jnp.int32),
        ),
        in_specs=[pl.BlockSpec(memory_space=pltpu.HBM)] * 6,
        out_specs=(whole, whole, whole),
        scratch_shapes=[
            [SMEM(v.shape, jnp.int32) for v in (a_support.T, b_support.T, retained, targets)],
            VMEM(a.shape, a.dtype),
            VMEM(b.shape, b.dtype),
            pltpu.SemaphoreType.DMA((6,)),
        ],
        compiler_params=pltpu.CompilerParams(vmem_limit_bytes=TIGHT),
        name="mask_factors",
    )(a_support.T, b_support.T, retained, targets, a, b)
    b_other = lax.ppermute(b_eff, "row", swap)
    half = n_col // 2
    far = n_col - 2
    pieces = {0: a_eff}
    for m, base in ((8, 0), (14, 0), (2, 0), (4, 0), (6, 0), (10, 8), (12, 8)):
        pieces[m] = across(pieces[base], m ^ base)
    late_even = [m for m in range(half + 2, far, 2)]
    late = range(late_even[0], late_even[-1] + 2)

    def exchanged(batch):
        return [m | 1 for m in batch], across(jnp.concatenate([pieces[m] for m in batch], axis=0), 1)

    early = [([m], pieces[m]) for m in sorted(pieces) if m not in late]
    early += [exchanged(batch) for batch in ((0, 2), (4,), (6, 8), (14,))]
    last = [([m], pieces[m]) for m in late_even] + [exchanged(late_even)]
    groups, shards = zip(*early)
    part, b_late = pl.pallas_call(
        functools.partial(gather_product_kernel, groups, late),
        out_shape=(
            jax.ShapeDtypeStruct((rows, columns), jnp.float32),
            jax.ShapeDtypeStruct((len(late) * EDGE, columns), b.dtype),
        ),
        in_specs=[whole] * (2 + len(groups)),
        out_specs=(whole, whole),
        compiler_params=params,
        cost_estimate=pl.CostEstimate(
            flops=2 * rows * columns * n_col * EDGE, bytes_accessed=8 * 1024 * 1024, transcendentals=0
        ),
        name="gather_product",
    )(b_eff, b_other, *shards)

    groups, shards = zip(*last)
    product, stats, codes = pl.pallas_call(
        functools.partial(inflate_kernel, groups),
        out_shape=(
            jax.ShapeDtypeStruct((rows, columns), jnp.float32),
            jax.ShapeDtypeStruct(((limit + 9) // 8 * 8, columns), jnp.float32),
            jax.ShapeDtypeStruct((limit, EDGE, EDGE), jnp.int16),
        ),
        in_specs=[whole] * (3 + len(groups)),
        out_specs=(whole, whole, whole),
        scratch_shapes=[SMEM(ints.shape, jnp.int32), pltpu.SemaphoreType.DMA],
        compiler_params=params,
        name="inflate",
    )(ints, part, b_late, *shards)

    other_stats = lax.ppermute(stats, "row", swap)
    arrived = lax.ppermute(codes, "row", swap)
    result, placed, step, scale = pl.pallas_call(
        functools.partial(finish_kernel, 2 * rows, limit),
        out_shape=(
            jax.ShapeDtypeStruct((rows, columns), jnp.bfloat16),
            jax.ShapeDtypeStruct((2 * limit, EDGE, EDGE), jnp.bfloat16),
            jax.ShapeDtypeStruct((limit, 1, EDGE), jnp.float32),
            jax.ShapeDtypeStruct((limit, 1, EDGE), jnp.float32),
        ),
        in_specs=[scalars] + [whole] * 3,
        out_specs=(whole,) * 4,
        compiler_params=params,
        name="finish",
    )(ints, product, stats, other_stats)
    values = (arrived.astype(jnp.float32) + HALF) * step
    values = (values * values * scale).astype(jnp.bfloat16)
    placed = lax.dynamic_update_slice(placed, values, ((1 - i) * limit, 0, 0))
    return result, placed.reshape(2 * limit * EDGE, EDGE)


def solution(mesh):
    n_row, n_col = mesh.shape["row"], mesh.shape["col"]
    paired = n_row == 2 and n_col >= 16 and n_col & (n_col - 1) == 0
    placed = (P("row", "col"),) * 5 + (P("row", "col", None, None),)
    return jax.shard_map(
        body_pair if paired else body_any,
        mesh=mesh,
        in_specs=placed,
        out_specs=(P("row", "col"), P("row", "col")),
        check_vma=False,
    )
```

```python
import functools

import jax
import jax.numpy as jnp
from jax import lax
from jax.experimental import pallas as pl
from jax.experimental.pallas import tpu as pltpu
from jax.sharding import PartitionSpec as P

EDGE = 128
VMEM = pltpu.VMEM
SMEM = pltpu.SMEM
LIMIT = 48 * 1024 * 1024
STEPS = 65535.0
HALF = 32768
TINY = 1e-23
TIGHT = 60 * 1024 * 1024


def squaring_pass(values, pattern):
    row_tiles, col_tiles = pattern.shape
    shaped = values.reshape(row_tiles, EDGE, col_tiles, EDGE)
    return (shaped * pattern[:, None, :, None].astype(values.dtype)).reshape(values.shape)


def berths(tile_count, bands):
    return max(2, (tile_count + bands - 1) // bands)


def body_any(a, b, a_support, b_support, retained, target_bands):
    a_whole = lax.all_gather(squaring_pass(a, a_support), "col", axis=1, tiled=True)
    b_whole = lax.all_gather(squaring_pass(b, b_support), "row", axis=0, tiled=True)
    product = jnp.dot(a_whole, b_whole, preferred_element_type=jnp.float32)
    inflated = squaring_pass(product * product, retained)
    totals = lax.psum(jnp.sum(inflated, axis=0), "row")
    bands = lax.axis_size("row")
    all_rows = inflated.shape[0] * bands
    result = (inflated / (totals / all_rows + 1e-05)).astype(jnp.bfloat16)
    tile_rows, tile_cols = retained.shape
    tile_count = tile_rows * tile_cols
    limit = berths(tile_count, bands)
    stack = result.reshape(tile_rows, EDGE, tile_cols, EDGE).transpose(0, 2, 1, 3)
    stack = stack.reshape(tile_count, EDGE * EDGE)
    targets = target_bands.reshape(tile_count)
    same_target = targets[:, None] == targets[None, :]
    earlier = jnp.arange(tile_count)[None, :] < jnp.arange(tile_count)[:, None]
    rank = jnp.sum((same_target & earlier).astype(jnp.int32), axis=1)
    position = targets * limit + rank
    selector = (jnp.arange(bands * limit)[:, None] == position[None, :]).astype(jnp.bfloat16)
    outgoing = jnp.dot(selector, stack, preferred_element_type=jnp.float32).astype(jnp.bfloat16)
    outgoing = outgoing.reshape(bands, limit, EDGE, EDGE)
    delivered = lax.all_to_all(outgoing, "row", split_axis=0, concat_axis=0, tiled=True)
    return result, delivered.reshape(bands * limit * EDGE, EDGE)


def mask_kernel(a_support, b_support, retained, targets, a, b, a_out, b_out, ints, keeps, a_local, b_local, sems):
    a_keep, b_keep, retained_local, targets_local = keeps
    rows, tiles, cols = a.shape[0] // EDGE, b.shape[0] // EDGE, b.shape[1] // EDGE
    copies = [
        pltpu.make_async_copy(source, local, sems.at[k])
        for k, (source, local) in enumerate(
            (
                (a_support, a_keep),
                (b_support, b_keep),
                (a, a_local),
                (b, b_local),
                (retained, retained_local),
                (targets, targets_local),
            )
        )
    ]
    for copy in copies:
        copy.start()
    j = lax.axis_index("col")
    copies[0].wait()
    copies[2].wait()
    for r in range(rows):
        band = slice(r * EDGE, (r + 1) * EDGE)
        a_out[band, :] = a_local[band, :] * a_keep[0, r].astype(jnp.float32).astype(a.dtype)
    copies[1].wait()
    copies[3].wait()
    for q in range(tiles):
        band = slice(q * EDGE, (q + 1) * EDGE)
        place = lax.bitwise_and(lax.bitwise_xor(j, q), tiles - 1)
        for c in range(cols):
            lanes = slice(c * EDGE, (c + 1) * EDGE)
            keep = b_keep[c, q].astype(jnp.float32).astype(b.dtype)
            b_out[place, :, lanes] = b_local[band, lanes] * keep
    copies[4].wait()
    copies[5].wait()
    count = rows * cols
    lane = lax.broadcasted_iota(jnp.int32, ints.shape, 1)
    row = jnp.zeros(ints.shape, jnp.int32)
    for t in range(count):
        row = jnp.where(lane == t, retained_local[t // cols, t % cols], row)
        row = jnp.where(lane == count + t, targets_local[0, t], row)
    ints[...] = row


def side_by_side(pieces, groups, rows):
    shards = {
        m: piece[k * rows:(k + 1) * rows, :] for piece, group in zip(pieces, groups) for k, m in enumerate(group)
    }
    return jnp.concatenate([shards[m] for m in sorted(shards)], axis=1)


def gather_product_kernel(groups, late, b_own, b_other, *refs):
    *pieces, product, b_late = refs
    tiles, _, columns = b_own.shape
    own_first = lax.axis_index("col") // tiles == lax.axis_index("row")
    for first, second, chosen in ((b_own, b_other, own_first), (b_other, b_own, jnp.logical_not(own_first))):

        @pl.when(chosen)
        def _():
            a = side_by_side(pieces, groups, product.shape[0])
            low, high = late[0] - tiles, late[-1] + 1 - tiles
            b = jnp.concatenate([first[...], second[:low], second[high:]], axis=0)
            product[...] = jnp.dot(a, b.reshape(a.shape[1], columns), preferred_element_type=jnp.float32)
            b_late[...] = second[low:high].reshape(b_late.shape)


def inflate_kernel(groups, ints_far, part, b_late, *refs):
    *pieces, product, stats, codes, ints, sem = refs
    lookup = pltpu.make_async_copy(ints_far, ints, sem)
    lookup.start()
    i = lax.axis_index("row")
    rows, cols = part.shape[0] // EDGE, part.shape[1] // EDGE
    count = rows * cols
    a = side_by_side(pieces, groups, part.shape[0])
    whole = part[...] + jnp.dot(a, b_late[...], preferred_element_type=jnp.float32)
    lookup.wait()
    tops = []
    for c in range(cols):
        lanes = pl.ds(c * EDGE, EDGE)
        total = top = None
        for r in range(rows):
            keep = ints[0, r * cols + c].astype(jnp.float32)
            tile = jnp.abs(whole[r * EDGE:(r + 1) * EDGE, c * EDGE:(c + 1) * EDGE]) * keep
            product[pl.ds(r * EDGE, EDGE), lanes] = tile
            stacked = tile.reshape(EDGE // 8, 8, EDGE)
            sums, peak = jnp.sum(stacked * stacked, axis=0), jnp.max(stacked, axis=0)
            total = sums if r == 0 else total + sums
            top = peak if r == 0 else jnp.maximum(top, peak)
        top = jnp.max(top, axis=0, keepdims=True)
        stats[pl.ds(0, 1), lanes] = jnp.sum(total, axis=0, keepdims=True)
        stats[pl.ds(1, 1), lanes] = top
        tops.append(jnp.where(top > TINY, STEPS / jnp.maximum(top, TINY), 0.0))
    if codes.shape[0] * 2 != count:
        codes[...] = jnp.full_like(codes, -HALF)
        stats[pl.ds(2, codes.shape[0]), :] = jnp.zeros((codes.shape[0], cols * EDGE), jnp.float32)
    column = lax.broadcasted_iota(jnp.int32, (1, cols * EDGE), 1) // EDGE
    sent = jnp.int32(0)
    for t in range(count):
        r, c = t // cols, t % cols
        leaves = ints[0, count + t] != i

        @pl.when(leaves)
        def _():
            tile = product[pl.ds(r * EDGE, EDGE), pl.ds(c * EDGE, EDGE)]
            steps = (tile * tops[c] + 0.5).astype(jnp.int32) - HALF
            codes[sent] = steps.astype(codes.dtype)
            stats[pl.ds(2 + sent, 1), :] = (column == c).astype(jnp.float32)

        sent = sent + leaves.astype(jnp.int32)


def finish_kernel(all_rows, limit, ints, product, own, other, result, placed, step, scale):
    rows, cols = product.shape[0] // EDGE, product.shape[1] // EDGE
    i = lax.axis_index("row")
    total = own[0:1, :] + other[0:1, :]
    inverse = 1.0 / (total / all_rows + 1e-05)
    top = other[1:2, :] / STEPS
    for s in range(limit):
        chosen = other[2 + s:3 + s, :]
        step[s] = sum((chosen * top)[:, c * EDGE:(c + 1) * EDGE] for c in range(cols))
        scale[s] = sum((chosen * inverse)[:, c * EDGE:(c + 1) * EDGE] for c in range(cols))
    if 2 * limit != rows * cols:
        placed[...] = jnp.zeros_like(placed)
    kept = jnp.int32(0)
    for t in range(rows * cols):
        r, c = t // cols, t % cols
        lanes = slice(c * EDGE, (c + 1) * EDGE)
        tile = product[r * EDGE:(r + 1) * EDGE, lanes]
        tile = (tile * tile * inverse[:, lanes]).astype(result.dtype)
        result[r * EDGE:(r + 1) * EDGE, lanes] = tile
        stays = ints[0, rows * cols + t] == i

        @pl.when(stays)
        def _():
            placed[i * limit + kept] = tile

        kept = kept + stays.astype(jnp.int32)


def body_pair(a, b, a_support, b_support, retained, target_bands):
    n_col = lax.axis_size("col")
    swap = [(0, 1), (1, 0)]
    i = lax.axis_index("row")
    rows, columns = a.shape[0], b.shape[1]
    tile_count = retained.shape[0] * retained.shape[1]
    limit = berths(tile_count, 2)

    def across(values, mask):
        return lax.ppermute(values, "col", [(k, k ^ mask) for k in range(n_col)])

    whole = pl.BlockSpec(memory_space=VMEM)
    scalars = pl.BlockSpec(memory_space=SMEM)
    params = pltpu.CompilerParams(vmem_limit_bytes=LIMIT)
    targets = target_bands.reshape(1, tile_count)
    a_eff, b_eff, ints = pl.pallas_call(
        mask_kernel,
        out_shape=(
            pltpu.VMEM(a.shape, a.dtype),
            pltpu.VMEM((b.shape[0] // EDGE, EDGE, columns), b.dtype),
            pltpu.VMEM((1, (2 * tile_count + EDGE - 1) // EDGE * EDGE), jnp.int32),
        ),
        in_specs=[pl.BlockSpec(memory_space=pltpu.HBM)] * 6,
        out_specs=(whole, whole, whole),
        scratch_shapes=[
            [SMEM(v.shape, jnp.int32) for v in (a_support.T, b_support.T, retained, targets)],
            VMEM(a.shape, a.dtype),
            VMEM(b.shape, b.dtype),
            pltpu.SemaphoreType.DMA((6,)),
        ],
        compiler_params=pltpu.CompilerParams(vmem_limit_bytes=TIGHT),
        name="mask_factors",
    )(a_support.T, b_support.T, retained, targets, a, b)
    b_other = lax.ppermute(b_eff, "row", swap)
    half = n_col // 2
    far = n_col - 2
    pieces = {0: a_eff}
    for m, base in ((8, 0), (14, 0), (2, 0), (4, 0), (6, 0), (10, 8), (12, 8)):
        pieces[m] = across(pieces[base], m ^ base)
    late_even = [m for m in range(half + 2, far, 2)]
    late = range(late_even[0], late_even[-1] + 2)

    def exchanged(batch):
        return [m | 1 for m in batch], across(jnp.concatenate([pieces[m] for m in batch], axis=0), 1)

    early = [([m], pieces[m]) for m in sorted(pieces) if m not in late]
    early += [exchanged(batch) for batch in ((0, 2, 4), (6, 8, 14))]
    *moved, b_other = lax.optimization_barrier((*[pieces[m] for m in late_even], b_other))
    pieces.update(zip(late_even, moved))
    last = [([m], pieces[m]) for m in late_even] + [exchanged(late_even)]
    groups, shards = zip(*early)
    part, b_late = pl.pallas_call(
        functools.partial(gather_product_kernel, groups, late),
        out_shape=(
            jax.ShapeDtypeStruct((rows, columns), jnp.float32),
            jax.ShapeDtypeStruct((len(late) * EDGE, columns), b.dtype),
        ),
        in_specs=[whole] * (2 + len(groups)),
        out_specs=(whole, whole),
        compiler_params=params,
        cost_estimate=pl.CostEstimate(
            flops=2 * rows * columns * n_col * EDGE, bytes_accessed=8 * 1024 * 1024, transcendentals=0
        ),
        name="gather_product",
    )(b_eff, b_other, *shards)

    groups, shards = zip(*last)
    product, stats, codes = pl.pallas_call(
        functools.partial(inflate_kernel, groups),
        out_shape=(
            jax.ShapeDtypeStruct((rows, columns), jnp.float32),
            jax.ShapeDtypeStruct(((limit + 9) // 8 * 8, columns), jnp.float32),
            jax.ShapeDtypeStruct((limit, EDGE, EDGE), jnp.int16),
        ),
        in_specs=[whole] * (3 + len(groups)),
        out_specs=(whole, whole, whole),
        scratch_shapes=[SMEM(ints.shape, jnp.int32), pltpu.SemaphoreType.DMA],
        compiler_params=params,
        name="inflate",
    )(ints, part, b_late, *shards)

    other_stats = lax.ppermute(stats, "row", swap)
    arrived = lax.ppermute(codes, "row", swap)
    result, placed, step, scale = pl.pallas_call(
        functools.partial(finish_kernel, 2 * rows, limit),
        out_shape=(
            jax.ShapeDtypeStruct((rows, columns), jnp.bfloat16),
            jax.ShapeDtypeStruct((2 * limit, EDGE, EDGE), jnp.bfloat16),
            jax.ShapeDtypeStruct((limit, 1, EDGE), jnp.float32),
            jax.ShapeDtypeStruct((limit, 1, EDGE), jnp.float32),
        ),
        in_specs=[scalars] + [whole] * 3,
        out_specs=(whole,) * 4,
        compiler_params=params,
        name="finish",
    )(ints, product, stats, other_stats)
    values = (arrived.astype(jnp.float32) + HALF) * step
    values = (values * values * scale).astype(jnp.bfloat16)
    placed = lax.dynamic_update_slice(placed, values, ((1 - i) * limit, 0, 0))
    return result, placed.reshape(2 * limit * EDGE, EDGE)


def solution(mesh):
    n_row, n_col = mesh.shape["row"], mesh.shape["col"]
    paired = n_row == 2 and n_col >= 16 and n_col & (n_col - 1) == 0
    placed = (P("row", "col"),) * 5 + (P("row", "col", None, None),)
    return jax.shard_map(
        body_pair if paired else body_any,
        mesh=mesh,
        in_specs=placed,
        out_specs=(P("row", "col"), P("row", "col")),
        check_vma=False,
    )
```

```python
import functools

import jax
import jax.numpy as jnp
from jax import lax
from jax.experimental import pallas as pl
from jax.experimental.pallas import tpu as pltpu
from jax.sharding import PartitionSpec as P

EDGE = 128
VMEM = pltpu.VMEM
SMEM = pltpu.SMEM
LIMIT = 48 * 1024 * 1024
STEPS = 65535.0
HALF = 32768
TINY = 1e-23
TIGHT = 60 * 1024 * 1024


def squaring_pass(values, pattern):
    row_tiles, col_tiles = pattern.shape
    shaped = values.reshape(row_tiles, EDGE, col_tiles, EDGE)
    return (shaped * pattern[:, None, :, None].astype(values.dtype)).reshape(values.shape)


def berths(tile_count, bands):
    return max(2, (tile_count + bands - 1) // bands)


def body_any(a, b, a_support, b_support, retained, target_bands):
    a_whole = lax.all_gather(squaring_pass(a, a_support), "col", axis=1, tiled=True)
    b_whole = lax.all_gather(squaring_pass(b, b_support), "row", axis=0, tiled=True)
    product = jnp.dot(a_whole, b_whole, preferred_element_type=jnp.float32)
    inflated = squaring_pass(product * product, retained)
    totals = lax.psum(jnp.sum(inflated, axis=0), "row")
    bands = lax.axis_size("row")
    all_rows = inflated.shape[0] * bands
    result = (inflated / (totals / all_rows + 1e-05)).astype(jnp.bfloat16)
    tile_rows, tile_cols = retained.shape
    tile_count = tile_rows * tile_cols
    limit = berths(tile_count, bands)
    stack = result.reshape(tile_rows, EDGE, tile_cols, EDGE).transpose(0, 2, 1, 3)
    stack = stack.reshape(tile_count, EDGE * EDGE)
    targets = target_bands.reshape(tile_count)
    same_target = targets[:, None] == targets[None, :]
    earlier = jnp.arange(tile_count)[None, :] < jnp.arange(tile_count)[:, None]
    rank = jnp.sum((same_target & earlier).astype(jnp.int32), axis=1)
    position = targets * limit + rank
    selector = (jnp.arange(bands * limit)[:, None] == position[None, :]).astype(jnp.bfloat16)
    outgoing = jnp.dot(selector, stack, preferred_element_type=jnp.float32).astype(jnp.bfloat16)
    outgoing = outgoing.reshape(bands, limit, EDGE, EDGE)
    delivered = lax.all_to_all(outgoing, "row", split_axis=0, concat_axis=0, tiled=True)
    return result, delivered.reshape(bands * limit * EDGE, EDGE)


def mask_kernel(a_support, b_support, retained, targets, a, b, a_out, b_out, ints, keeps, a_local, b_local, sems):
    a_keep, b_keep, retained_local, targets_local = keeps
    rows, tiles, cols = a.shape[0] // EDGE, b.shape[0] // EDGE, b.shape[1] // EDGE
    copies = [
        pltpu.make_async_copy(source, local, sems.at[k])
        for k, (source, local) in enumerate(
            (
                (a_support, a_keep),
                (b_support, b_keep),
                (a, a_local),
                (b, b_local),
                (retained, retained_local),
                (targets, targets_local),
            )
        )
    ]
    for copy in copies:
        copy.start()
    j = lax.axis_index("col")
    copies[0].wait()
    copies[2].wait()
    for r in range(rows):
        band = slice(r * EDGE, (r + 1) * EDGE)
        a_out[band, :] = a_local[band, :] * a_keep[0, r].astype(jnp.float32).astype(a.dtype)
    copies[1].wait()
    copies[3].wait()
    for q in range(tiles):
        band = slice(q * EDGE, (q + 1) * EDGE)
        place = lax.bitwise_and(lax.bitwise_xor(j, q), tiles - 1)
        for c in range(cols):
            lanes = slice(c * EDGE, (c + 1) * EDGE)
            keep = b_keep[c, q].astype(jnp.float32).astype(b.dtype)
            b_out[place, :, lanes] = b_local[band, lanes] * keep
    copies[4].wait()
    copies[5].wait()
    count = rows * cols
    lane = lax.broadcasted_iota(jnp.int32, ints.shape, 1)
    row = jnp.zeros(ints.shape, jnp.int32)
    for t in range(count):
        row = jnp.where(lane == t, retained_local[t // cols, t % cols], row)
        row = jnp.where(lane == count + t, targets_local[0, t], row)
    ints[...] = row


def side_by_side(pieces, groups, rows):
    shards = {
        m: piece[k * rows:(k + 1) * rows, :] for piece, group in zip(pieces, groups) for k, m in enumerate(group)
    }
    return jnp.concatenate([shards[m] for m in sorted(shards)], axis=1)


def gather_product_kernel(groups, late, b_own, b_other, *refs):
    *pieces, product, b_late = refs
    tiles, _, columns = b_own.shape
    own_first = lax.axis_index("col") // tiles == lax.axis_index("row")
    for first, second, chosen in ((b_own, b_other, own_first), (b_other, b_own, jnp.logical_not(own_first))):

        @pl.when(chosen)
        def _():
            a = side_by_side(pieces, groups, product.shape[0])
            low, high = late[0] - tiles, late[-1] + 1 - tiles
            b = jnp.concatenate([first[...], second[:low], second[high:]], axis=0)
            product[...] = jnp.dot(a, b.reshape(a.shape[1], columns), preferred_element_type=jnp.float32)
            b_late[...] = second[low:high].reshape(b_late.shape)


def inflate_kernel(groups, ints_far, part, b_late, *refs):
    *pieces, product, stats, codes, ints, sem = refs
    lookup = pltpu.make_async_copy(ints_far, ints, sem)
    lookup.start()
    i = lax.axis_index("row")
    rows, cols = part.shape[0] // EDGE, part.shape[1] // EDGE
    count = rows * cols
    a = side_by_side(pieces, groups, part.shape[0])
    whole = part[...] + jnp.dot(a, b_late[...], preferred_element_type=jnp.float32)
    lookup.wait()
    tops = []
    for c in range(cols):
        lanes = pl.ds(c * EDGE, EDGE)
        total = top = None
        for r in range(rows):
            keep = ints[0, r * cols + c].astype(jnp.float32)
            tile = jnp.abs(whole[r * EDGE:(r + 1) * EDGE, c * EDGE:(c + 1) * EDGE]) * keep
            product[pl.ds(r * EDGE, EDGE), lanes] = tile
            stacked = tile.reshape(EDGE // 8, 8, EDGE)
            sums, peak = jnp.sum(stacked * stacked, axis=0), jnp.max(stacked, axis=0)
            total = sums if r == 0 else total + sums
            top = peak if r == 0 else jnp.maximum(top, peak)
        top = jnp.max(top, axis=0, keepdims=True)
        stats[pl.ds(0, 1), lanes] = jnp.sum(total, axis=0, keepdims=True)
        stats[pl.ds(1, 1), lanes] = top
        tops.append(jnp.where(top > TINY, STEPS / jnp.maximum(top, TINY), 0.0))
    if codes.shape[0] * 2 != count:
        codes[...] = jnp.full_like(codes, -HALF)
        stats[pl.ds(2, codes.shape[0]), :] = jnp.zeros((codes.shape[0], cols * EDGE), jnp.float32)
    column = lax.broadcasted_iota(jnp.int32, (1, cols * EDGE), 1) // EDGE
    sent = jnp.int32(0)
    for t in range(count):
        r, c = t // cols, t % cols
        leaves = ints[0, count + t] != i

        @pl.when(leaves)
        def _():
            tile = product[pl.ds(r * EDGE, EDGE), pl.ds(c * EDGE, EDGE)]
            steps = (tile * tops[c] + 0.5).astype(jnp.int32) - HALF
            codes[sent] = steps.astype(codes.dtype)
            stats[pl.ds(2 + sent, 1), :] = (column == c).astype(jnp.float32)

        sent = sent + leaves.astype(jnp.int32)


def finish_kernel(all_rows, limit, ints, product, own, other, result, placed, step, scale):
    rows, cols = product.shape[0] // EDGE, product.shape[1] // EDGE
    i = lax.axis_index("row")
    total = own[0:1, :] + other[0:1, :]
    inverse = 1.0 / (total / all_rows + 1e-05)
    top = other[1:2, :] / STEPS
    for s in range(limit):
        chosen = other[2 + s:3 + s, :]
        step[s] = sum((chosen * top)[:, c * EDGE:(c + 1) * EDGE] for c in range(cols))
        scale[s] = sum((chosen * inverse)[:, c * EDGE:(c + 1) * EDGE] for c in range(cols))
    if 2 * limit != rows * cols:
        placed[...] = jnp.zeros_like(placed)
    kept = jnp.int32(0)
    for t in range(rows * cols):
        r, c = t // cols, t % cols
        lanes = slice(c * EDGE, (c + 1) * EDGE)
        tile = product[r * EDGE:(r + 1) * EDGE, lanes]
        tile = (tile * tile * inverse[:, lanes]).astype(result.dtype)
        result[r * EDGE:(r + 1) * EDGE, lanes] = tile
        stays = ints[0, rows * cols + t] == i

        @pl.when(stays)
        def _():
            placed[i * limit + kept] = tile

        kept = kept + stays.astype(jnp.int32)


def body_pair(a, b, a_support, b_support, retained, target_bands):
    n_col = lax.axis_size("col")
    swap = [(0, 1), (1, 0)]
    i = lax.axis_index("row")
    rows, columns = a.shape[0], b.shape[1]
    tile_count = retained.shape[0] * retained.shape[1]
    limit = berths(tile_count, 2)

    def across(values, mask):
        return lax.ppermute(values, "col", [(k, k ^ mask) for k in range(n_col)])

    whole = pl.BlockSpec(memory_space=VMEM)
    scalars = pl.BlockSpec(memory_space=SMEM)
    params = pltpu.CompilerParams(vmem_limit_bytes=LIMIT)
    targets = target_bands.reshape(1, tile_count)
    a_eff, b_eff, ints = pl.pallas_call(
        mask_kernel,
        out_shape=(
            pltpu.VMEM(a.shape, a.dtype),
            pltpu.VMEM((b.shape[0] // EDGE, EDGE, columns), b.dtype),
            pltpu.VMEM((1, (2 * tile_count + EDGE - 1) // EDGE * EDGE), jnp.int32),
        ),
        in_specs=[pl.BlockSpec(memory_space=pltpu.HBM)] * 6,
        out_specs=(whole, whole, whole),
        scratch_shapes=[
            [SMEM(v.shape, jnp.int32) for v in (a_support.T, b_support.T, retained, targets)],
            VMEM(a.shape, a.dtype),
            VMEM(b.shape, b.dtype),
            pltpu.SemaphoreType.DMA((6,)),
        ],
        compiler_params=pltpu.CompilerParams(vmem_limit_bytes=TIGHT),
        name="mask_factors",
    )(a_support.T, b_support.T, retained, targets, a, b)
    b_other = lax.ppermute(b_eff, "row", swap)
    half = n_col // 2
    far = n_col - 2
    pieces = {0: a_eff}
    for m in (half, far, *range(2, half, 2)):
        pieces[m] = across(a_eff, m)
    late_even = list(range(half + 2, far, 2))
    for m in late_even:
        pieces[m] = across(pieces[half], m ^ half)
    late = range(late_even[0], late_even[-1] + 2)
    batches = list(range(0, half - 2, 2)), [half - 2, half, far]

    def exchanged(batch):
        return [m | 1 for m in batch], across(jnp.concatenate([pieces[m] for m in batch], axis=0), 1)

    early = [([m], pieces[m]) for m in sorted(pieces) if m not in late]
    early += [exchanged(batch) for batch in batches]
    *moved, b_other = lax.optimization_barrier((*[pieces[m] for m in late_even], b_other))
    pieces.update(zip(late_even, moved))
    last = [([m], pieces[m]) for m in late_even] + [exchanged(late_even)]
    groups, shards = zip(*early)
    part, b_late = pl.pallas_call(
        functools.partial(gather_product_kernel, groups, late),
        out_shape=(
            jax.ShapeDtypeStruct((rows, columns), jnp.float32),
            jax.ShapeDtypeStruct((len(late) * EDGE, columns), b.dtype),
        ),
        in_specs=[whole] * (2 + len(groups)),
        out_specs=(whole, whole),
        compiler_params=params,
        cost_estimate=pl.CostEstimate(
            flops=2 * rows * columns * n_col * EDGE, bytes_accessed=8 * 1024 * 1024, transcendentals=0
        ),
        name="gather_product",
    )(b_eff, b_other, *shards)

    groups, shards = zip(*last)
    product, stats, codes = pl.pallas_call(
        functools.partial(inflate_kernel, groups),
        out_shape=(
            jax.ShapeDtypeStruct((rows, columns), jnp.float32),
            jax.ShapeDtypeStruct(((limit + 9) // 8 * 8, columns), jnp.float32),
            jax.ShapeDtypeStruct((limit, EDGE, EDGE), jnp.int16),
        ),
        in_specs=[whole] * (3 + len(groups)),
        out_specs=(whole, whole, whole),
        scratch_shapes=[SMEM(ints.shape, jnp.int32), pltpu.SemaphoreType.DMA],
        compiler_params=params,
        name="inflate",
    )(ints, part, b_late, *shards)

    other_stats = lax.ppermute(stats, "row", swap)
    arrived = lax.ppermute(codes, "row", swap)
    result, placed, step, scale = pl.pallas_call(
        functools.partial(finish_kernel, 2 * rows, limit),
        out_shape=(
            jax.ShapeDtypeStruct((rows, columns), jnp.bfloat16),
            jax.ShapeDtypeStruct((2 * limit, EDGE, EDGE), jnp.bfloat16),
            jax.ShapeDtypeStruct((limit, 1, EDGE), jnp.float32),
            jax.ShapeDtypeStruct((limit, 1, EDGE), jnp.float32),
        ),
        in_specs=[scalars] + [whole] * 3,
        out_specs=(whole,) * 4,
        compiler_params=params,
        name="finish",
    )(ints, product, stats, other_stats)
    values = (arrived.astype(jnp.float32) + HALF) * step
    values = (values * values * scale).astype(jnp.bfloat16)
    placed = lax.dynamic_update_slice(placed, values, ((1 - i) * limit, 0, 0))
    return result, placed.reshape(2 * limit * EDGE, EDGE)


def solution(mesh):
    n_row, n_col = mesh.shape["row"], mesh.shape["col"]

    def body(a, b, *supports):
        fits = n_row == 2 and n_col >= 16 and n_col & (n_col - 1) == 0
        fits = fits and a.shape[1] == EDGE and 2 * b.shape[0] == n_col * EDGE
        return (body_pair if fits else body_any)(a, b, *supports)

    placed = (P("row", "col"),) * 5 + (P("row", "col", None, None),)
    return jax.shard_map(
        body,
        mesh=mesh,
        in_specs=placed,
        out_specs=(P("row", "col"), P("row", "col")),
        check_vma=False,
    )
```

```python
import functools

import jax
import jax.numpy as jnp
from jax import lax
from jax.experimental import pallas as pl
from jax.experimental.pallas import tpu as pltpu
from jax.sharding import PartitionSpec as P

EDGE = 128
VMEM = pltpu.VMEM
SMEM = pltpu.SMEM
LIMIT = 48 * 1024 * 1024
STEPS = 65535.0
HALF = 32768
TINY = 1e-23
TIGHT = 60 * 1024 * 1024


def squaring_pass(values, pattern):
    row_tiles, col_tiles = pattern.shape
    shaped = values.reshape(row_tiles, EDGE, col_tiles, EDGE)
    return (shaped * pattern[:, None, :, None].astype(values.dtype)).reshape(values.shape)


def berths(tile_count, bands):
    return max(2, (tile_count + bands - 1) // bands)


def body_any(a, b, a_support, b_support, retained, target_bands):
    a_whole = lax.all_gather(squaring_pass(a, a_support), "col", axis=1, tiled=True)
    b_whole = lax.all_gather(squaring_pass(b, b_support), "row", axis=0, tiled=True)
    product = jnp.dot(a_whole, b_whole, preferred_element_type=jnp.float32)
    inflated = squaring_pass(product * product, retained)
    totals = lax.psum(jnp.sum(inflated, axis=0), "row")
    bands = lax.axis_size("row")
    all_rows = inflated.shape[0] * bands
    result = (inflated / (totals / all_rows + 1e-05)).astype(jnp.bfloat16)
    tile_rows, tile_cols = retained.shape
    tile_count = tile_rows * tile_cols
    limit = berths(tile_count, bands)
    stack = result.reshape(tile_rows, EDGE, tile_cols, EDGE).transpose(0, 2, 1, 3)
    stack = stack.reshape(tile_count, EDGE * EDGE)
    targets = target_bands.reshape(tile_count)
    same_target = targets[:, None] == targets[None, :]
    earlier = jnp.arange(tile_count)[None, :] < jnp.arange(tile_count)[:, None]
    rank = jnp.sum((same_target & earlier).astype(jnp.int32), axis=1)
    position = targets * limit + rank
    selector = (jnp.arange(bands * limit)[:, None] == position[None, :]).astype(jnp.bfloat16)
    outgoing = jnp.dot(selector, stack, preferred_element_type=jnp.float32).astype(jnp.bfloat16)
    outgoing = outgoing.reshape(bands, limit, EDGE, EDGE)
    delivered = lax.all_to_all(outgoing, "row", split_axis=0, concat_axis=0, tiled=True)
    return result, delivered.reshape(bands * limit * EDGE, EDGE)


def mask_kernel(a_support, b_support, retained, targets, a, b, a_out, b_out, ints, keeps, a_local, b_local, sems):
    a_keep, b_keep, retained_local, targets_local = keeps
    rows, tiles, cols = a.shape[0] // EDGE, b.shape[0] // EDGE, b.shape[1] // EDGE
    copies = [
        pltpu.make_async_copy(source, local, sems.at[k])
        for k, (source, local) in enumerate(
            (
                (a_support, a_keep),
                (b_support, b_keep),
                (a, a_local),
                (b, b_local),
                (retained, retained_local),
                (targets, targets_local),
            )
        )
    ]
    for copy in copies:
        copy.start()
    j = lax.axis_index("col")
    copies[0].wait()
    copies[2].wait()
    for r in range(rows):
        band = slice(r * EDGE, (r + 1) * EDGE)
        a_out[band, :] = a_local[band, :] * a_keep[0, r].astype(jnp.float32).astype(a.dtype)
    copies[1].wait()
    copies[3].wait()
    for q in range(tiles):
        band = slice(q * EDGE, (q + 1) * EDGE)
        place = lax.bitwise_and(lax.bitwise_xor(j, q), tiles - 1)
        for c in range(cols):
            lanes = slice(c * EDGE, (c + 1) * EDGE)
            keep = b_keep[c, q].astype(jnp.float32).astype(b.dtype)
            b_out[place, :, lanes] = b_local[band, lanes] * keep
    copies[4].wait()
    copies[5].wait()
    count = rows * cols
    lane = lax.broadcasted_iota(jnp.int32, ints.shape, 1)
    row = jnp.zeros(ints.shape, jnp.int32)
    for t in range(count):
        row = jnp.where(lane == t, retained_local[t // cols, t % cols], row)
        row = jnp.where(lane == count + t, targets_local[0, t], row)
    ints[...] = row


def side_by_side(pieces, groups, rows):
    shards = {
        m: piece[k * rows:(k + 1) * rows, :] for piece, group in zip(pieces, groups) for k, m in enumerate(group)
    }
    return jnp.concatenate([shards[m] for m in sorted(shards)], axis=1)


def gather_product_kernel(groups, late, b_own, b_other, *refs):
    *pieces, product, b_late = refs
    tiles, _, columns = b_own.shape
    own_first = lax.axis_index("col") // tiles == lax.axis_index("row")
    for first, second, chosen in ((b_own, b_other, own_first), (b_other, b_own, jnp.logical_not(own_first))):

        @pl.when(chosen)
        def _():
            a = side_by_side(pieces, groups, product.shape[0])
            low, high = late[0] - tiles, late[-1] + 1 - tiles
            b = jnp.concatenate([first[...], second[:low], second[high:]], axis=0)
            product[...] = jnp.dot(a, b.reshape(a.shape[1], columns), preferred_element_type=jnp.float32)
            b_late[...] = second[low:high].reshape(b_late.shape)


def inflate_kernel(groups, ints_far, part, b_late, *refs):
    *pieces, product, stats, codes, ints, sem = refs
    lookup = pltpu.make_async_copy(ints_far, ints, sem)
    lookup.start()
    i = lax.axis_index("row")
    rows, cols = part.shape[0] // EDGE, part.shape[1] // EDGE
    count = rows * cols
    a = side_by_side(pieces, groups, part.shape[0])
    pairs = []
    for at in range(0, cols, 2):
        lanes = slice(at * EDGE, min(at + 2, cols) * EDGE)
        pairs.append(part[:, lanes] + jnp.dot(a, b_late[:, lanes], preferred_element_type=jnp.float32))
    lookup.wait()
    tops = []
    for c in range(cols):
        lanes = pl.ds(c * EDGE, EDGE)
        total = top = None
        for r in range(rows):
            keep = ints[0, r * cols + c].astype(jnp.float32)
            tile = pairs[c // 2][r * EDGE:(r + 1) * EDGE, c % 2 * EDGE:(c % 2 + 1) * EDGE]
            tile = jnp.abs(tile) * keep
            product[pl.ds(r * EDGE, EDGE), lanes] = tile
            stacked = tile.reshape(EDGE // 8, 8, EDGE)
            sums, peak = jnp.sum(stacked * stacked, axis=0), jnp.max(stacked, axis=0)
            total = sums if r == 0 else total + sums
            top = peak if r == 0 else jnp.maximum(top, peak)
        top = jnp.max(top, axis=0, keepdims=True)
        stats[pl.ds(0, 1), lanes] = jnp.sum(total, axis=0, keepdims=True)
        stats[pl.ds(1, 1), lanes] = top
        tops.append(jnp.where(top > TINY, STEPS / jnp.maximum(top, TINY), 0.0))
    if codes.shape[0] * 2 != count:
        codes[...] = jnp.full_like(codes, -HALF)
        stats[pl.ds(2, codes.shape[0]), :] = jnp.zeros((codes.shape[0], cols * EDGE), jnp.float32)
    column = lax.broadcasted_iota(jnp.int32, (1, cols * EDGE), 1) // EDGE
    sent = jnp.int32(0)
    for t in range(count):
        r, c = t // cols, t % cols
        leaves = ints[0, count + t] != i

        @pl.when(leaves)
        def _():
            tile = product[pl.ds(r * EDGE, EDGE), pl.ds(c * EDGE, EDGE)]
            steps = (tile * tops[c] + 0.5).astype(jnp.int32) - HALF
            codes[sent] = steps.astype(codes.dtype)
            stats[pl.ds(2 + sent, 1), :] = (column == c).astype(jnp.float32)

        sent = sent + leaves.astype(jnp.int32)


def finish_kernel(all_rows, limit, ints, product, own, other, result, placed, step, scale):
    rows, cols = product.shape[0] // EDGE, product.shape[1] // EDGE
    i = lax.axis_index("row")
    total = own[0:1, :] + other[0:1, :]
    inverse = 1.0 / (total / all_rows + 1e-05)
    top = other[1:2, :] / STEPS
    for s in range(limit):
        chosen = other[2 + s:3 + s, :]
        step[s] = sum((chosen * top)[:, c * EDGE:(c + 1) * EDGE] for c in range(cols))
        scale[s] = sum((chosen * inverse)[:, c * EDGE:(c + 1) * EDGE] for c in range(cols))
    if 2 * limit != rows * cols:
        placed[...] = jnp.zeros_like(placed)
    kept = jnp.int32(0)
    for t in range(rows * cols):
        r, c = t // cols, t % cols
        lanes = slice(c * EDGE, (c + 1) * EDGE)
        tile = product[r * EDGE:(r + 1) * EDGE, lanes]
        tile = (tile * tile * inverse[:, lanes]).astype(result.dtype)
        result[r * EDGE:(r + 1) * EDGE, lanes] = tile
        stays = ints[0, rows * cols + t] == i

        @pl.when(stays)
        def _():
            placed[i * limit + kept] = tile

        kept = kept + stays.astype(jnp.int32)


def body_pair(a, b, a_support, b_support, retained, target_bands):
    n_col = lax.axis_size("col")
    swap = [(0, 1), (1, 0)]
    i = lax.axis_index("row")
    rows, columns = a.shape[0], b.shape[1]
    tile_count = retained.shape[0] * retained.shape[1]
    limit = berths(tile_count, 2)

    def across(values, mask):
        return lax.ppermute(values, "col", [(k, k ^ mask) for k in range(n_col)])

    whole = pl.BlockSpec(memory_space=VMEM)
    scalars = pl.BlockSpec(memory_space=SMEM)
    params = pltpu.CompilerParams(vmem_limit_bytes=LIMIT)
    targets = target_bands.reshape(1, tile_count)
    a_eff, b_eff, ints = pl.pallas_call(
        mask_kernel,
        out_shape=(
            pltpu.VMEM(a.shape, a.dtype),
            pltpu.VMEM((b.shape[0] // EDGE, EDGE, columns), b.dtype),
            pltpu.VMEM((1, (2 * tile_count + EDGE - 1) // EDGE * EDGE), jnp.int32),
        ),
        in_specs=[pl.BlockSpec(memory_space=pltpu.HBM)] * 6,
        out_specs=(whole, whole, whole),
        scratch_shapes=[
            [SMEM(v.shape, jnp.int32) for v in (a_support.T, b_support.T, retained, targets)],
            VMEM(a.shape, a.dtype),
            VMEM(b.shape, b.dtype),
            pltpu.SemaphoreType.DMA((6,)),
        ],
        compiler_params=pltpu.CompilerParams(vmem_limit_bytes=TIGHT),
        name="mask_factors",
    )(a_support.T, b_support.T, retained, targets, a, b)
    b_other = lax.ppermute(b_eff, "row", swap)
    half = n_col // 2
    far = n_col - 2
    pieces = {0: a_eff}
    for m in (half, far, *range(2, half, 2)):
        pieces[m] = across(a_eff, m)
    late_even = list(range(half + 2, far, 2))
    for m in late_even:
        pieces[m] = across(pieces[half], m ^ half)
    late = range(late_even[0], late_even[-1] + 2)
    batches = list(range(0, half - 2, 2)), [half - 2, half, far]

    def exchanged(batch):
        return [m | 1 for m in batch], across(jnp.concatenate([pieces[m] for m in batch], axis=0), 1)

    early = [([m], pieces[m]) for m in sorted(pieces) if m not in late]
    early += [exchanged(batch) for batch in batches]
    *moved, b_other = lax.optimization_barrier((*[pieces[m] for m in late_even], b_other))
    pieces.update(zip(late_even, moved))
    last = [([m], pieces[m]) for m in late_even] + [exchanged(late_even)]
    groups, shards = zip(*early)
    part, b_late = pl.pallas_call(
        functools.partial(gather_product_kernel, groups, late),
        out_shape=(
            jax.ShapeDtypeStruct((rows, columns), jnp.float32),
            jax.ShapeDtypeStruct((len(late) * EDGE, columns), b.dtype),
        ),
        in_specs=[whole] * (2 + len(groups)),
        out_specs=(whole, whole),
        compiler_params=params,
        cost_estimate=pl.CostEstimate(
            flops=2 * rows * columns * n_col * EDGE, bytes_accessed=8 * 1024 * 1024, transcendentals=0
        ),
        name="gather_product",
    )(b_eff, b_other, *shards)

    groups, shards = zip(*last)
    product, stats, codes = pl.pallas_call(
        functools.partial(inflate_kernel, groups),
        out_shape=(
            jax.ShapeDtypeStruct((rows, columns), jnp.float32),
            jax.ShapeDtypeStruct(((limit + 9) // 8 * 8, columns), jnp.float32),
            jax.ShapeDtypeStruct((limit, EDGE, EDGE), jnp.int16),
        ),
        in_specs=[whole] * (3 + len(groups)),
        out_specs=(whole, whole, whole),
        scratch_shapes=[SMEM(ints.shape, jnp.int32), pltpu.SemaphoreType.DMA],
        compiler_params=params,
        name="inflate",
    )(ints, part, b_late, *shards)

    other_stats = lax.ppermute(stats, "row", swap)
    arrived = lax.ppermute(codes, "row", swap)
    result, placed, step, scale = pl.pallas_call(
        functools.partial(finish_kernel, 2 * rows, limit),
        out_shape=(
            jax.ShapeDtypeStruct((rows, columns), jnp.bfloat16),
            jax.ShapeDtypeStruct((2 * limit, EDGE, EDGE), jnp.bfloat16),
            jax.ShapeDtypeStruct((limit, 1, EDGE), jnp.float32),
            jax.ShapeDtypeStruct((limit, 1, EDGE), jnp.float32),
        ),
        in_specs=[scalars] + [whole] * 3,
        out_specs=(whole,) * 4,
        compiler_params=params,
        name="finish",
    )(ints, product, stats, other_stats)
    values = (arrived.astype(jnp.float32) + HALF) * step
    values = (values * values * scale).astype(jnp.bfloat16)
    placed = lax.dynamic_update_slice(placed, values, ((1 - i) * limit, 0, 0))
    return result, placed.reshape(2 * limit * EDGE, EDGE)


def solution(mesh):
    n_row, n_col = mesh.shape["row"], mesh.shape["col"]

    def body(a, b, *supports):
        fits = n_row == 2 and n_col >= 16 and n_col & (n_col - 1) == 0
        fits = fits and a.shape[1] == EDGE and 2 * b.shape[0] == n_col * EDGE
        return (body_pair if fits else body_any)(a, b, *supports)

    placed = (P("row", "col"),) * 5 + (P("row", "col", None, None),)
    return jax.shard_map(
        body,
        mesh=mesh,
        in_specs=placed,
        out_specs=(P("row", "col"), P("row", "col")),
        check_vma=False,
    )
```

```python
import functools

import jax
import jax.numpy as jnp
from jax import lax
from jax.experimental import pallas as pl
from jax.experimental.pallas import tpu as pltpu
from jax.sharding import PartitionSpec as P

EDGE = 128
VMEM = pltpu.VMEM
SMEM = pltpu.SMEM
LIMIT = 48 * 1024 * 1024
STEPS = 65535.0
HALF = 32768
TINY = 1e-23
TIGHT = 60 * 1024 * 1024


def squaring_pass(values, pattern):
    row_tiles, col_tiles = pattern.shape
    shaped = values.reshape(row_tiles, EDGE, col_tiles, EDGE)
    return (shaped * pattern[:, None, :, None].astype(values.dtype)).reshape(values.shape)


def berths(tile_count, bands):
    return max(2, (tile_count + bands - 1) // bands)


def body_any(a, b, a_support, b_support, retained, target_bands):
    a_whole = lax.all_gather(squaring_pass(a, a_support), "col", axis=1, tiled=True)
    b_whole = lax.all_gather(squaring_pass(b, b_support), "row", axis=0, tiled=True)
    product = jnp.dot(a_whole, b_whole, preferred_element_type=jnp.float32)
    inflated = squaring_pass(product * product, retained)
    totals = lax.psum(jnp.sum(inflated, axis=0), "row")
    bands = lax.axis_size("row")
    all_rows = inflated.shape[0] * bands
    result = (inflated / (totals / all_rows + 1e-05)).astype(jnp.bfloat16)
    tile_rows, tile_cols = retained.shape
    tile_count = tile_rows * tile_cols
    limit = berths(tile_count, bands)
    stack = result.reshape(tile_rows, EDGE, tile_cols, EDGE).transpose(0, 2, 1, 3)
    stack = stack.reshape(tile_count, EDGE * EDGE)
    targets = target_bands.reshape(tile_count)
    same_target = targets[:, None] == targets[None, :]
    earlier = jnp.arange(tile_count)[None, :] < jnp.arange(tile_count)[:, None]
    rank = jnp.sum((same_target & earlier).astype(jnp.int32), axis=1)
    position = targets * limit + rank
    selector = (jnp.arange(bands * limit)[:, None] == position[None, :]).astype(jnp.bfloat16)
    outgoing = jnp.dot(selector, stack, preferred_element_type=jnp.float32).astype(jnp.bfloat16)
    outgoing = outgoing.reshape(bands, limit, EDGE, EDGE)
    delivered = lax.all_to_all(outgoing, "row", split_axis=0, concat_axis=0, tiled=True)
    return result, delivered.reshape(bands * limit * EDGE, EDGE)


def mask_kernel(a_support, b_support, retained, targets, a, b, a_out, b_out, ints, keeps, a_local, b_local, sems):
    a_keep, b_keep, retained_local, targets_local = keeps
    rows, tiles, cols = a.shape[0] // EDGE, b.shape[0] // EDGE, b.shape[1] // EDGE
    middle = tiles // 2 * EDGE
    copies = [
        pltpu.make_async_copy(source, local, sems.at[k])
        for k, (source, local) in enumerate(
            (
                (a_support, a_keep),
                (b_support, b_keep),
                (a, a_local),
                (b.at[:middle, :], b_local.at[:middle, :]),
                (retained, retained_local),
                (targets, targets_local),
                (b.at[middle:, :], b_local.at[middle:, :]),
            )
        )
    ]
    for copy in copies:
        copy.start()
    j = lax.axis_index("col")
    copies[0].wait()
    copies[2].wait()
    for r in range(rows):
        band = slice(r * EDGE, (r + 1) * EDGE)
        a_out[band, :] = a_local[band, :] * a_keep[0, r].astype(jnp.float32).astype(a.dtype)
    copies[1].wait()
    copies[3].wait()
    for q in range(tiles):
        if q * EDGE == middle:
            copies[6].wait()
        band = slice(q * EDGE, (q + 1) * EDGE)
        place = lax.bitwise_and(lax.bitwise_xor(j, q), tiles - 1)
        for c in range(cols):
            lanes = slice(c * EDGE, (c + 1) * EDGE)
            keep = b_keep[c, q].astype(jnp.float32).astype(b.dtype)
            b_out[place, :, lanes] = b_local[band, lanes] * keep
    copies[4].wait()
    copies[5].wait()
    count = rows * cols
    lane = lax.broadcasted_iota(jnp.int32, ints.shape, 1)
    row = jnp.zeros(ints.shape, jnp.int32)
    for t in range(count):
        row = jnp.where(lane == t, retained_local[t // cols, t % cols], row)
        row = jnp.where(lane == count + t, targets_local[0, t], row)
    ints[...] = row


def side_by_side(pieces, groups, rows):
    shards = {
        m: piece[k * rows:(k + 1) * rows, :] for piece, group in zip(pieces, groups) for k, m in enumerate(group)
    }
    return jnp.concatenate([shards[m] for m in sorted(shards)], axis=1)


def gather_product_kernel(groups, late, b_own, b_other, *refs):
    *pieces, product, b_late = refs
    tiles, _, columns = b_own.shape
    own_first = lax.axis_index("col") // tiles == lax.axis_index("row")
    for first, second, chosen in ((b_own, b_other, own_first), (b_other, b_own, jnp.logical_not(own_first))):

        @pl.when(chosen)
        def _():
            a = side_by_side(pieces, groups, product.shape[0])
            low, high = late[0] - tiles, late[-1] + 1 - tiles
            b = jnp.concatenate([first[...], second[:low], second[high:]], axis=0)
            product[...] = jnp.dot(a, b.reshape(a.shape[1], columns), preferred_element_type=jnp.float32)
            b_late[...] = second[low:high].reshape(b_late.shape)


def inflate_kernel(groups, ints_far, part, b_late, *refs):
    *pieces, product, stats, codes, ints, sem = refs
    lookup = pltpu.make_async_copy(ints_far, ints, sem)
    lookup.start()
    i = lax.axis_index("row")
    rows, cols = part.shape[0] // EDGE, part.shape[1] // EDGE
    count = rows * cols
    a = side_by_side(pieces, groups, part.shape[0])
    whole = part[...] + jnp.dot(a, b_late[...], preferred_element_type=jnp.float32)
    lookup.wait()
    tops = []
    for c in range(cols):
        lanes = pl.ds(c * EDGE, EDGE)
        total = top = None
        for r in range(rows):
            keep = ints[0, r * cols + c].astype(jnp.float32)
            tile = jnp.abs(whole[r * EDGE:(r + 1) * EDGE, c * EDGE:(c + 1) * EDGE]) * keep
            product[pl.ds(r * EDGE, EDGE), lanes] = tile
            stacked = tile.reshape(EDGE // 8, 8, EDGE)
            sums, peak = jnp.sum(stacked * stacked, axis=0), jnp.max(stacked, axis=0)
            total = sums if r == 0 else total + sums
            top = peak if r == 0 else jnp.maximum(top, peak)
        top = jnp.max(top, axis=0, keepdims=True)
        stats[pl.ds(0, 1), lanes] = jnp.sum(total, axis=0, keepdims=True)
        stats[pl.ds(1, 1), lanes] = top
        tops.append(jnp.where(top > TINY, STEPS / jnp.maximum(top, TINY), 0.0))
    if codes.shape[0] * 2 != count:
        codes[...] = jnp.full_like(codes, -HALF)
        stats[pl.ds(2, codes.shape[0]), :] = jnp.zeros((codes.shape[0], cols * EDGE), jnp.float32)
    column = lax.broadcasted_iota(jnp.int32, (1, cols * EDGE), 1) // EDGE
    sent = jnp.int32(0)
    for t in range(count):
        r, c = t // cols, t % cols
        leaves = ints[0, count + t] != i

        @pl.when(leaves)
        def _():
            tile = product[pl.ds(r * EDGE, EDGE), pl.ds(c * EDGE, EDGE)]
            steps = (tile * tops[c] + 0.5).astype(jnp.int32) - HALF
            codes[sent] = steps.astype(codes.dtype)
            stats[pl.ds(2 + sent, 1), :] = (column == c).astype(jnp.float32)

        sent = sent + leaves.astype(jnp.int32)


def finish_kernel(all_rows, limit, ints, product, own, other, result, placed, step, scale):
    rows, cols = product.shape[0] // EDGE, product.shape[1] // EDGE
    i = lax.axis_index("row")
    total = own[0:1, :] + other[0:1, :]
    inverse = 1.0 / (total / all_rows + 1e-05)
    top = other[1:2, :] / STEPS
    for s in range(limit):
        chosen = other[2 + s:3 + s, :]
        step[s] = sum((chosen * top)[:, c * EDGE:(c + 1) * EDGE] for c in range(cols))
        scale[s] = sum((chosen * inverse)[:, c * EDGE:(c + 1) * EDGE] for c in range(cols))
    if 2 * limit != rows * cols:
        placed[...] = jnp.zeros_like(placed)
    kept = jnp.int32(0)
    for t in range(rows * cols):
        r, c = t // cols, t % cols
        lanes = slice(c * EDGE, (c + 1) * EDGE)
        tile = product[r * EDGE:(r + 1) * EDGE, lanes]
        tile = (tile * tile * inverse[:, lanes]).astype(result.dtype)
        result[r * EDGE:(r + 1) * EDGE, lanes] = tile
        stays = ints[0, rows * cols + t] == i

        @pl.when(stays)
        def _():
            placed[i * limit + kept] = tile

        kept = kept + stays.astype(jnp.int32)


def body_pair(a, b, a_support, b_support, retained, target_bands):
    n_col = lax.axis_size("col")
    swap = [(0, 1), (1, 0)]
    i = lax.axis_index("row")
    rows, columns = a.shape[0], b.shape[1]
    tile_count = retained.shape[0] * retained.shape[1]
    limit = berths(tile_count, 2)

    def across(values, mask):
        return lax.ppermute(values, "col", [(k, k ^ mask) for k in range(n_col)])

    whole = pl.BlockSpec(memory_space=VMEM)
    scalars = pl.BlockSpec(memory_space=SMEM)
    params = pltpu.CompilerParams(vmem_limit_bytes=LIMIT)
    targets = target_bands.reshape(1, tile_count)
    a_eff, b_eff, ints = pl.pallas_call(
        mask_kernel,
        out_shape=(
            pltpu.VMEM(a.shape, a.dtype),
            pltpu.VMEM((b.shape[0] // EDGE, EDGE, columns), b.dtype),
            pltpu.VMEM((1, (2 * tile_count + EDGE - 1) // EDGE * EDGE), jnp.int32),
        ),
        in_specs=[pl.BlockSpec(memory_space=pltpu.HBM)] * 6,
        out_specs=(whole, whole, whole),
        scratch_shapes=[
            [SMEM(v.shape, jnp.int32) for v in (a_support.T, b_support.T, retained, targets)],
            VMEM(a.shape, a.dtype),
            VMEM(b.shape, b.dtype),
            pltpu.SemaphoreType.DMA((7,)),
        ],
        compiler_params=pltpu.CompilerParams(vmem_limit_bytes=TIGHT),
        name="mask_factors",
    )(a_support.T, b_support.T, retained, targets, a, b)
    b_other = lax.ppermute(b_eff, "row", swap)
    half = n_col // 2
    far = n_col - 2
    pieces = {0: a_eff}
    for m in (half, far, *range(2, half, 2)):
        pieces[m] = across(a_eff, m)
    late_even = list(range(half + 2, far, 2))
    for m in late_even:
        pieces[m] = across(pieces[half], m ^ half)
    late = range(late_even[0], late_even[-1] + 2)
    batches = list(range(0, half - 2, 2)), [half - 2, half, far]

    def exchanged(batch):
        return [m | 1 for m in batch], across(jnp.concatenate([pieces[m] for m in batch], axis=0), 1)

    early = [([m], pieces[m]) for m in sorted(pieces) if m not in late]
    early += [exchanged(batch) for batch in batches]
    *moved, b_other = lax.optimization_barrier((*[pieces[m] for m in late_even], b_other))
    pieces.update(zip(late_even, moved))
    last = [([m], pieces[m]) for m in late_even] + [exchanged(late_even)]
    groups, shards = zip(*early)
    part, b_late = pl.pallas_call(
        functools.partial(gather_product_kernel, groups, late),
        out_shape=(
            jax.ShapeDtypeStruct((rows, columns), jnp.float32),
            jax.ShapeDtypeStruct((len(late) * EDGE, columns), b.dtype),
        ),
        in_specs=[whole] * (2 + len(groups)),
        out_specs=(whole, whole),
        compiler_params=params,
        cost_estimate=pl.CostEstimate(
            flops=2 * rows * columns * n_col * EDGE, bytes_accessed=8 * 1024 * 1024, transcendentals=0
        ),
        name="gather_product",
    )(b_eff, b_other, *shards)

    groups, shards = zip(*last)
    product, stats, codes = pl.pallas_call(
        functools.partial(inflate_kernel, groups),
        out_shape=(
            jax.ShapeDtypeStruct((rows, columns), jnp.float32),
            jax.ShapeDtypeStruct(((limit + 9) // 8 * 8, columns), jnp.float32),
            jax.ShapeDtypeStruct((limit, EDGE, EDGE), jnp.int16),
        ),
        in_specs=[whole] * (3 + len(groups)),
        out_specs=(whole, whole, whole),
        scratch_shapes=[SMEM(ints.shape, jnp.int32), pltpu.SemaphoreType.DMA],
        compiler_params=params,
        name="inflate",
    )(ints, part, b_late, *shards)

    other_stats = lax.ppermute(stats, "row", swap)
    arrived = lax.ppermute(codes, "row", swap)
    result, placed, step, scale = pl.pallas_call(
        functools.partial(finish_kernel, 2 * rows, limit),
        out_shape=(
            jax.ShapeDtypeStruct((rows, columns), jnp.bfloat16),
            jax.ShapeDtypeStruct((2 * limit, EDGE, EDGE), jnp.bfloat16),
            jax.ShapeDtypeStruct((limit, 1, EDGE), jnp.float32),
            jax.ShapeDtypeStruct((limit, 1, EDGE), jnp.float32),
        ),
        in_specs=[scalars] + [whole] * 3,
        out_specs=(whole,) * 4,
        compiler_params=params,
        name="finish",
    )(ints, product, stats, other_stats)
    values = (arrived.astype(jnp.float32) + HALF) * step
    values = (values * values * scale).astype(jnp.bfloat16)
    placed = lax.dynamic_update_slice(placed, values, ((1 - i) * limit, 0, 0))
    return result, placed.reshape(2 * limit * EDGE, EDGE)


def solution(mesh):
    n_row, n_col = mesh.shape["row"], mesh.shape["col"]

    def body(a, b, *supports):
        fits = n_row == 2 and n_col >= 16 and n_col & (n_col - 1) == 0
        fits = fits and a.shape[1] == EDGE and 2 * b.shape[0] == n_col * EDGE
        return (body_pair if fits else body_any)(a, b, *supports)

    placed = (P("row", "col"),) * 5 + (P("row", "col", None, None),)
    return jax.shard_map(
        body,
        mesh=mesh,
        in_specs=placed,
        out_specs=(P("row", "col"), P("row", "col")),
        check_vma=False,
    )
```
